128 devices in a mesh: outer: 16 (over z, y), narrow: 8 (over x, core).
Axes of the slice: x: 4, y: 4, z: 4, core: 2. Of those that a mesh axis runs over, the one named last changes fastest.
Arguments:
- queries: bfloat16 [32768, 4096], P(('outer', 'narrow')), may hold values from -6 to 6
- keys: bfloat16 [32768, 4096], P(('outer', 'narrow')), may hold values from -6 to 6
- values: bfloat16 [32768, 4096], P(('outer', 'narrow')), may hold values from -6 to 6
- log_decay: float32 [32, 32768], P(None, ('outer', 'narrow')), may hold values from -0.8 to 0
- gain: float32 [4096], replicated, may hold values from 0.5 to 1.5
Outputs:
- mixed: bfloat16 [32768, 4096], P(('outer', 'narrow'))
The draws below stay inside these ranges and needn't reach their ends.
All inputs are finite; a program needn't handle non-finite values.
Results may differ from the reference program's by a relative error of at most 0.0052.
Values may be sent and summed in bfloat16 or wider, within the bound.
No kernel may reach another device: no remote copies, remote signals or barrier semaphores. Data moves between devices by JAX's collectives and lax.ppermute only.
A program may use at most 64 MiB of HBM per device.

```python
import jax
import jax.numpy as jnp
from jax import lax

HEAD_COUNT = 32
DH = 128
TOK_DEV = 256
D = 4096
SPAN_LENGTH = 32768


def draw_log_decay(key, part):
    segments = jax.random.split(jax.random.fold_in(key, 17), 7)
    share = 0.5
    fast = jax.random.uniform(segments[0], (HEAD_COUNT,), jnp.float32) < share
    horizon = jnp.exp(jax.random.uniform(segments[1], (HEAD_COUNT,), jnp.float32, jnp.log(30.0), jnp.log(50.0)))
    slow_total = jax.random.uniform(segments[2], (HEAD_COUNT,), jnp.float32, 0.1, 0.3)
    base = jnp.where(fast, -1.0 / horizon, -slow_total / SPAN_LENGTH)
    count = SPAN_LENGTH // TOK_DEV
    block_factor = jnp.exp(jax.random.uniform(segments[3], (HEAD_COUNT, count), jnp.float32, jnp.log(0.5), jnp.log(2.0)))
    block_factor = jnp.repeat(block_factor, TOK_DEV, axis=1)
    place_factor = jax.random.uniform(segments[4], (HEAD_COUNT, SPAN_LENGTH), jnp.float32, 0.5, 1.5)
    forget_speeds = base[:, None] * block_factor * place_factor
    spike_indices = jax.random.randint(segments[5], (HEAD_COUNT, 2), 0, SPAN_LENGTH)
    forget_falls = jax.random.uniform(segments[6], (HEAD_COUNT, 2), jnp.float32, jnp.log(0.5), jnp.log(0.8))
    spike_finder = jnp.arange(SPAN_LENGTH)[None, None, :] == spike_indices[:, :, None]
    forget_spikes = jnp.sum(jnp.where(spike_finder, forget_falls[:, :, None], 0.0), axis=1)
    return (forget_speeds + forget_spikes).astype(jnp.float32)


def block_levels(key, extent, shards, least, largest):
    factor_of, own = 1.0, jax.random.fold_in(key, 6)
    for axis_at, shards_of in shards:
        steps = jnp.exp(jax.random.uniform(jax.random.fold_in(own, axis_at), (shards_of,), jnp.float32, least / len(shards), largest / len(shards)))
        factor_of = factor_of * jnp.repeat(steps, extent[axis_at] // shards_of).reshape([-1 if axis == axis_at else 1 for axis in range(len(extent))])
    return factor_of


def scatter_about(key, dims, scale, reach, pieces=(), kind=jnp.bfloat16):
    array = scale * jax.random.normal(key, dims, jnp.float32)
    if pieces:
        array = array * block_levels(key, dims, pieces, -0.22, 0.18)
    return jnp.clip(array, -reach, reach).astype(kind)


def setup_inputs(seed: int = 0) -> dict:
    key_list = jax.random.split(jax.random.key(seed), 6)
    queries = scatter_about(key_list[0], (SPAN_LENGTH, D), 1.0, 6.0, ((0, 128),))
    keys = scatter_about(key_list[1], (SPAN_LENGTH, D), 1.0, 6.0, ((0, 128),))
    values = scatter_about(key_list[2], (SPAN_LENGTH, D), 1.0, 6.0, ((0, 128),))
    log_decay = draw_log_decay(jax.random.fold_in(key_list[5], 71), 0)
    gain = jnp.clip(1.0 + 0.1 * jax.random.normal(key_list[4], (D,), jnp.float32), 0.5, 1.5)
    return {"queries": queries, "keys": keys, "values": values, "log_decay": log_decay, "gain": gain}


def reference(queries, keys, values, log_decay, gain):
    blocks = queries.shape[0] // TOK_DEV
    qall = queries.reshape(blocks, TOK_DEV, HEAD_COUNT, DH)
    kall = keys.reshape(blocks, TOK_DEV, HEAD_COUNT, DH)
    vall = values.reshape(blocks, TOK_DEV, HEAD_COUNT, DH)
    decay_all = jnp.transpose(log_decay.reshape(HEAD_COUNT, blocks, TOK_DEV), (1, 0, 2))
    gains = gain.reshape(HEAD_COUNT, DH)
    causal = jnp.arange(TOK_DEV)[:, None] >= jnp.arange(TOK_DEV)[None, :]

    def step(state, inputs):
        qblk, kblk, vblk, forget_speeds = inputs
        cum = jnp.cumsum(forget_speeds, axis=1)
        total = cum[:, -1]
        factor = jnp.exp(total[:, None] - cum).T
        decayed = (kblk.astype(jnp.float32) * factor[:, :, None]).astype(jnp.bfloat16)
        block_state = jnp.einsum('thd,the->hde', decayed.astype(jnp.float32), vblk.astype(jnp.float32))
        half = state.astype(jnp.bfloat16)
        scores = jnp.einsum('thd,shd->hts', qblk.astype(jnp.float32), kblk.astype(jnp.float32))
        spread = jnp.minimum(cum[:, :, None] - cum[:, None, :], 0.0)
        weights = jnp.where(causal[None], scores * jnp.exp(spread), 0.0).astype(jnp.bfloat16)
        inner = jnp.einsum('hts,she->the', weights.astype(jnp.float32), vblk.astype(jnp.float32))
        readout = jnp.einsum('thd,hde->the', qblk.astype(jnp.float32), half.astype(jnp.float32))
        numer = inner + readout * jnp.exp(cum).T[:, :, None]
        scale = lax.rsqrt(lax.optimization_barrier(jnp.mean(numer * numer, axis=-1, keepdims=True)) + 1e-06)
        result = (numer * scale * gains[None]).astype(jnp.bfloat16)
        fresh = jnp.exp(total)[:, None, None] * state + block_state
        return (fresh, result.reshape(TOK_DEV, HEAD_COUNT * DH))
    start = jnp.zeros((HEAD_COUNT, DH, DH), jnp.float32)
    final, outputs = lax.scan(step, start, (qall, kall, vall, decay_all))
    return outputs.reshape(blocks * TOK_DEV, HEAD_COUNT * DH)
```

```python
import functools

import jax
import jax.numpy as jnp
from jax import lax
from jax.experimental import pallas as pl
from jax.experimental.pallas import tpu as pltpu
from jax.sharding import Mesh
from jax.sharding import PartitionSpec as P

BF = jnp.bfloat16
F32 = jnp.float32
CHIPS = ("z", "y", "x")
ALL = ("z", "y", "x", "c")
HB = 8
W = 128
T = 256
HALF = 16
SPLIT = 48
ROWS = 40
MB = 1 << 20


def running(x):
    lane = lax.broadcasted_iota(jnp.int32, x.shape, 1)
    step = 1
    while step < x.shape[1]:
        x = x + jnp.where(lane >= step, pltpu.roll(x, step, axis=1), 0.0)
        step *= 2
    return x


def split3(x):
    hi = x.astype(BF).astype(F32)
    mid = (x - hi).astype(BF).astype(F32)
    return hi, mid, x - hi - mid


def dot(a, b, dims=((1,), (0,))):
    return lax.dot_general(a, b, (dims, ((), ())), preferred_element_type=F32)


def state_step(ld_ref, k_ref, v_ref):
    cum = running(ld_ref[...])
    total = cum[:, T - 1 :]
    factor = jnp.exp(total - cum)

    def state(j):
        kt = k_ref[:, j * W : (j + 1) * W].T
        decayed = (kt.astype(F32) * factor[j : j + 1, :]).astype(BF)
        return dot(decayed, v_ref[:, j * W : (j + 1) * W])

    return jnp.exp(total), state


def send_states(core_ref, ld_ref, k_ref, v_ref, out_ref):
    i = pl.program_id(0)
    decay, state = state_step(ld_ref, k_ref, v_ref)
    for j in range(HB):
        out_ref[pl.ds(pl.multiple_of(i * HB * W + j * W, W), W), :] = state(j).astype(BF)
    wide = jnp.broadcast_to(decay, (HB, W))
    first = HALF * W

    @pl.when(i == 0)
    def _():
        out_ref[first:, :] = jnp.zeros((SPLIT, W), BF)

    place = lax.broadcasted_iota(jnp.int32, (HALF, W), 0) // HB == i
    both = jnp.concatenate([wide, wide], axis=0)
    for n, term in enumerate(split3(both)):
        rows = slice(first + n * HALF, first + (n + 1) * HALF)
        old = out_ref[rows, :].astype(F32)
        out_ref[rows, :] = jnp.where(place, term, old).astype(BF)


def own_states(core_ref, ld_ref, k_ref, v_ref, out_ref, decay_ref):
    decay, state = state_step(ld_ref, k_ref, v_ref)
    for j in range(HB):
        out_ref[j] = state(j)
    decay_ref[...] = jnp.broadcast_to(decay, (HB, W))


def other_decay(recv_ref):
    first = HALF * W
    terms = [recv_ref[first + n * HALF : first + (n + 1) * HALF, :].astype(F32) for n in range(3)]
    return terms[0] + terms[1] + terms[2]


def combine(core_ref, own_ref, decay_ref, recv_ref, out_ref):
    here = decay_ref[...]
    there = other_decay(recv_ref)
    earlier = core_ref[0] == 0
    one = jnp.ones_like(here)
    a_own = jnp.where(earlier, there, one)
    a_recv = jnp.where(earlier, one, here)
    terms = split3(here * there)
    zeros = jnp.zeros((ROWS - 32 - 3, W), F32)
    for h in range(HALF):
        tail = jnp.concatenate([t[h : h + 1] for t in terms] + [zeros], axis=0)
        for r in range(4):
            own = own_ref[h, r * 32 : (r + 1) * 32, :]
            recv = recv_ref[h * W + r * 32 : h * W + (r + 1) * 32, :].astype(F32)
            body = a_own[h : h + 1] * own + a_recv[h : h + 1] * recv
            out_ref[4 * h + r] = jnp.concatenate([body, tail], axis=0).astype(BF)


def scan_chips(in_ref, out_ref):
    carry = jnp.zeros((32, W), F32)
    for j in range(in_ref.shape[0]):
        out_ref[j] = carry.astype(BF)
        x = in_ref[j].astype(F32)
        decay = x[32:33] + x[33:34] + x[34:35]
        carry = decay * carry + x[:32]


def spread_back(core_ref, chip_ref, own_ref, decay_ref, recv_ref, keep_ref, send_ref):
    earlier = core_ref[0] == 0
    decay = jnp.where(earlier, decay_ref[...], other_decay(recv_ref))
    for h in range(HALF):
        for r in range(4):
            rows = slice(r * 32, (r + 1) * 32)
            first = chip_ref[4 * h + r].astype(F32)
            own = own_ref[h, rows, :]
            recv = recv_ref[h * W + r * 32 : h * W + (r + 1) * 32, :].astype(F32)
            second = decay[h : h + 1] * first + jnp.where(earlier, own, recv)
            keep_ref[h, rows, :] = jnp.where(earlier, first, second).astype(BF)
            send_ref[h, rows, :] = jnp.where(earlier, second, first).astype(BF)


def within(ld_ref, q_ref, k_ref, v_ref, out_ref):
    cum = running(ld_ref[...])
    cols = cum.T
    n = W
    causal = lax.broadcasted_iota(jnp.int32, (n, n), 0) >= lax.broadcasted_iota(jnp.int32, (n, n), 1)
    for j in range(HB):
        at = slice(j * W, (j + 1) * W)
        row = cum[j : j + 1, :]
        col = jnp.broadcast_to(cols[:, j : j + 1], (T, n))

        def piece(t, s):
            scores = dot(q_ref[t * n : (t + 1) * n, at], k_ref[s * n : (s + 1) * n, at], ((1,), (1,)))
            gap = col[t * n : (t + 1) * n] - row[:, s * n : (s + 1) * n]
            weights = scores * jnp.exp(jnp.minimum(gap, 0.0))
            if t == s:
                weights = jnp.where(causal, weights, 0.0)
            return weights.astype(BF)

        out_ref[:n, at] = dot(piece(0, 0), v_ref[:n, at])
        lower = jnp.concatenate([piece(1, 0), piece(1, 1)], axis=1)
        out_ref[n:, at] = dot(lower, v_ref[:, at])


def finish_step(ld_ref, q_ref, inner_ref, carried_ref, gain_ref, out_ref):
    grown = jnp.exp(running(ld_ref[...])).T
    for j in range(HB):
        at = slice(j * W, (j + 1) * W)
        readout = dot(q_ref[:, at], carried_ref[j])
        numer = inner_ref[:, at] + readout * grown[:, j : j + 1]
        mean = jnp.mean(numer * numer, axis=1, keepdims=True)
        scale = lax.rsqrt(mean + 1e-6)
        out_ref[:, at] = (numer * scale * gain_ref[:, at]).astype(BF)


def finish_own(core_ref, *refs):
    finish_step(*refs)


def finish_other(core_ref, old_ref, *refs):
    finish_step(*refs)


def cost(flops, bytes_accessed):
    return pl.CostEstimate(flops=flops, bytes_accessed=bytes_accessed, transcendentals=0)


def params():
    return pltpu.CompilerParams(vmem_limit_bytes=40 * MB)


def on_device(queries, keys, values, log_decay, gain):
    core = lax.axis_index("c")
    which = core.astype(jnp.int32).reshape(1)
    heads = log_decay.shape[0]
    chips = HALF * 4

    def own(i, c):
        return c[0] * (HALF // HB) + i

    def other(i, c):
        return (1 - c[0]) * (HALF // HB) + i

    def per_half(kernel, group, ins, outs, shapes, **kw):
        return pl.pallas_call(
            kernel,
            grid_spec=pltpu.PrefetchScalarGridSpec(
                num_scalar_prefetch=1,
                grid=(HALF // HB,),
                in_specs=[s(group) for s in ins],
                out_specs=[s(group) for s in outs],
            ),
            out_shape=shapes,
            compiler_params=params(),
            **kw,
        )

    def tokens(group):
        return pl.BlockSpec((T, HB * W), lambda i, c: (0, group(i, c)))

    def decays(group):
        return pl.BlockSpec((HB, T), lambda i, c: (group(i, c), 0))

    def gains(group):
        return pl.BlockSpec((1, HB * W), lambda i, c: (0, group(i, c)))

    def states(group):
        return pl.BlockSpec((HB, W, W), lambda i, c: (i, 0, 0))

    def small(group):
        return pl.BlockSpec((HB, W), lambda i, c: (i, 0))

    def whole(group):
        return pl.BlockSpec((HALF * W + SPLIT, W), lambda i, c: (0, 0))

    swap = functools.partial(lax.ppermute, axis_name="c", perm=[(0, 1), (1, 0)])
    sent_shape = jax.ShapeDtypeStruct((HALF * W + SPLIT, W), BF)
    [sent] = per_half(
        send_states, other, [decays, tokens, tokens], [whole], [sent_shape],
        cost_estimate=cost(1 << 27, 3 * MB),
    )(which, log_decay, keys, values)
    recv = swap(sent)
    state, decay = per_half(
        own_states, own, [decays, tokens, tokens], [states, small],
        [jax.ShapeDtypeStruct((HALF, W, W), F32), jax.ShapeDtypeStruct((HALF, W), F32)],
        cost_estimate=cost(1 << 27, 3 * MB),
    )(which, log_decay, keys, values)
    smem = pl.BlockSpec(memory_space=pltpu.SMEM)
    vmem = pl.BlockSpec(memory_space=pltpu.VMEM)
    chunks = pl.pallas_call(
        combine,
        in_specs=[smem, vmem, vmem, vmem],
        out_specs=vmem,
        out_shape=jax.ShapeDtypeStruct((chips, ROWS, W), BF),
        compiler_params=params(),
    )(which, state, decay, recv)
    owned = lax.all_to_all(chunks, CHIPS, split_axis=0, concat_axis=0, tiled=True)
    before = pl.pallas_call(
        scan_chips,
        in_specs=[vmem],
        out_specs=vmem,
        out_shape=jax.ShapeDtypeStruct((chips, 32, W), BF),
        compiler_params=params(),
    )(owned)
    inner = pl.pallas_call(
        within,
        grid=(heads // HB,),
        in_specs=[pl.BlockSpec((HB, T), lambda i: (i, 0))]
        + [pl.BlockSpec((T, HB * W), lambda i: (0, i))] * 3,
        out_specs=pl.BlockSpec((T, HB * W), lambda i: (0, i)),
        out_shape=jax.ShapeDtypeStruct((T, heads * W), F32),
        compiler_params=params(),
        cost_estimate=cost(1 << 31, 10 * MB),
    )(log_decay, queries, keys, values)
    back = lax.all_to_all(before, CHIPS, split_axis=0, concat_axis=0, tiled=True)
    keep, give = pl.pallas_call(
        spread_back,
        in_specs=[smem, vmem, vmem, vmem, vmem],
        out_specs=[vmem, vmem],
        out_shape=[jax.ShapeDtypeStruct((HALF, W, W), BF)] * 2,
        compiler_params=params(),
    )(which, back, state, decay, recv)
    taken = swap(give)
    gain_row = gain.reshape(1, heads * W)
    out_shape = jax.ShapeDtypeStruct((T, heads * W), BF)
    [first] = per_half(
        finish_own, own, [decays, tokens, tokens, states, gains], [tokens], [out_shape],
        cost_estimate=cost(1 << 27, 5 * MB),
    )(which, log_decay, queries, inner, keep, gain_row)

    def left_alone(group):
        return pl.BlockSpec(memory_space=pl.ANY)

    [out] = per_half(
        finish_other, other, [left_alone, decays, tokens, tokens, states, gains], [tokens], [out_shape],
        input_output_aliases={1: 0},
        cost_estimate=cost(1 << 27, 5 * MB),
    )(which, first, log_decay, queries, inner, taken, gain_row)
    return out


def solution(mesh):
    chips = Mesh(mesh.devices.reshape(4, 4, 4, 2), ALL)
    placed = (P(ALL, None), P(ALL, None), P(ALL, None), P(None, ALL), P())
    return jax.shard_map(on_device, mesh=chips, in_specs=placed, out_specs=P(ALL, None), check_vma=False)
```

```python
import functools

import jax
import jax.numpy as jnp
from jax import lax
from jax.experimental import pallas as pl
from jax.experimental.pallas import tpu as pltpu
from jax.sharding import Mesh
from jax.sharding import PartitionSpec as P

BF = jnp.bfloat16
F32 = jnp.float32
CHIPS = ("z", "y", "x")
ALL = ("z", "y", "x", "c")
HB = 8
W = 128
T = 256
HALF = 16
SPLIT = 48
ROWS = 40
MB = 1 << 20


def running(x):
    lane = lax.broadcasted_iota(jnp.int32, x.shape, 1)
    step = 1
    while step < x.shape[1]:
        x = x + jnp.where(lane >= step, pltpu.roll(x, step, axis=1), 0.0)
        step *= 2
    return x


def split3(x):
    hi = x.astype(BF).astype(F32)
    mid = (x - hi).astype(BF).astype(F32)
    return hi, mid, x - hi - mid


def dot(a, b, dims=((1,), (0,))):
    return lax.dot_general(a, b, (dims, ((), ())), preferred_element_type=F32)


def state_step(ld_ref, k_ref, v_ref):
    cum = running(ld_ref[...])
    total = cum[:, T - 1 :]
    factor = jnp.exp(total - cum)

    def state(j):
        kt = k_ref[:, j * W : (j + 1) * W].T
        decayed = (kt.astype(F32) * factor[j : j + 1, :]).astype(BF)
        return dot(decayed, v_ref[:, j * W : (j + 1) * W])

    return jnp.exp(total), state


def send_states(core_ref, ld_ref, k_ref, v_ref, out_ref):
    i = pl.program_id(0)
    decay, state = state_step(ld_ref, k_ref, v_ref)
    for j in range(HB):
        out_ref[pl.ds(pl.multiple_of(i * HB * W + j * W, W), W), :] = state(j).astype(BF)
    wide = jnp.broadcast_to(decay, (HB, W))
    first = HALF * W

    @pl.when(i == 0)
    def _():
        out_ref[first:, :] = jnp.zeros((SPLIT, W), BF)

    place = lax.broadcasted_iota(jnp.int32, (HALF, W), 0) // HB == i
    both = jnp.concatenate([wide, wide], axis=0)
    for n, term in enumerate(split3(both)):
        rows = slice(first + n * HALF, first + (n + 1) * HALF)
        old = out_ref[rows, :].astype(F32)
        out_ref[rows, :] = jnp.where(place, term, old).astype(BF)


def own_states(core_ref, ld_ref, k_ref, v_ref, out_ref, decay_ref):
    decay, state = state_step(ld_ref, k_ref, v_ref)
    for j in range(HB):
        out_ref[j] = state(j)
    decay_ref[...] = jnp.broadcast_to(decay, (HB, W))


def other_decay(recv_ref):
    first = HALF * W
    terms = [recv_ref[first + n * HALF : first + (n + 1) * HALF, :].astype(F32) for n in range(3)]
    return terms[0] + terms[1] + terms[2]


def combine(core_ref, own_ref, decay_ref, recv_ref, out_ref):
    here = decay_ref[...]
    there = other_decay(recv_ref)
    earlier = core_ref[0] == 0
    one = jnp.ones_like(here)
    a_own = jnp.where(earlier, there, one)
    a_recv = jnp.where(earlier, one, here)
    terms = split3(here * there)
    zeros = jnp.zeros((ROWS - 32 - 3, W), F32)
    for h in range(HALF):
        tail = jnp.concatenate([t[h : h + 1] for t in terms] + [zeros], axis=0)
        for r in range(4):
            own = own_ref[h, r * 32 : (r + 1) * 32, :]
            recv = recv_ref[h * W + r * 32 : h * W + (r + 1) * 32, :].astype(F32)
            body = a_own[h : h + 1] * own + a_recv[h : h + 1] * recv
            out_ref[4 * h + r] = jnp.concatenate([body, tail], axis=0).astype(BF)


def scan_chips(in_ref, out_ref):
    carry = jnp.zeros((32, W), F32)
    for j in range(in_ref.shape[0]):
        out_ref[j] = carry.astype(BF)
        x = in_ref[j].astype(F32)
        decay = x[32:33] + x[33:34] + x[34:35]
        carry = decay * carry + x[:32]


def spread_back(core_ref, chip_ref, own_ref, decay_ref, recv_ref, keep_ref, send_ref):
    earlier = core_ref[0] == 0
    decay = jnp.where(earlier, decay_ref[...], other_decay(recv_ref))
    for h in range(HALF):
        for r in range(4):
            rows = slice(r * 32, (r + 1) * 32)
            first = chip_ref[4 * h + r].astype(F32)
            own = own_ref[h, rows, :]
            recv = recv_ref[h * W + r * 32 : h * W + (r + 1) * 32, :].astype(F32)
            second = decay[h : h + 1] * first + jnp.where(earlier, own, recv)
            keep_ref[h, rows, :] = jnp.where(earlier, first, second).astype(BF)
            send_ref[h, rows, :] = jnp.where(earlier, second, first).astype(BF)


def within(ld_ref, q_ref, k_ref, v_ref, out_ref):
    cum = running(ld_ref[...])
    cols = cum.T
    n = W
    causal = lax.broadcasted_iota(jnp.int32, (n, n), 0) >= lax.broadcasted_iota(jnp.int32, (n, n), 1)
    for j in range(HB):
        at = slice(j * W, (j + 1) * W)
        row = cum[j : j + 1, :]
        col = jnp.broadcast_to(cols[:, j : j + 1], (T, n))

        def piece(t, s):
            scores = dot(q_ref[t * n : (t + 1) * n, at], k_ref[s * n : (s + 1) * n, at], ((1,), (1,)))
            gap = col[t * n : (t + 1) * n] - row[:, s * n : (s + 1) * n]
            weights = scores * jnp.exp(jnp.minimum(gap, 0.0))
            if t == s:
                weights = jnp.where(causal, weights, 0.0)
            return weights.astype(BF)

        out_ref[:n, at] = dot(piece(0, 0), v_ref[:n, at])
        lower = jnp.concatenate([piece(1, 0), piece(1, 1)], axis=1)
        out_ref[n:, at] = dot(lower, v_ref[:, at])


def finish_step(ld_ref, q_ref, inner_ref, carried_ref, gain_ref, out_ref):
    grown = jnp.exp(running(ld_ref[...])).T
    for j in range(HB):
        at = slice(j * W, (j + 1) * W)
        readout = dot(q_ref[:, at], carried_ref[j])
        numer = inner_ref[:, at] + readout * grown[:, j : j + 1]
        mean = jnp.mean(numer * numer, axis=1, keepdims=True)
        scale = lax.rsqrt(mean + 1e-6)
        out_ref[:, at] = (numer * scale * gain_ref[:, at]).astype(BF)


def finish_own(core_ref, *refs):
    finish_step(*refs)


def finish_other(core_ref, old_ref, *refs):
    finish_step(*refs)


def cost(flops, bytes_accessed):
    return pl.CostEstimate(flops=flops, bytes_accessed=bytes_accessed, transcendentals=0)


def params():
    return pltpu.CompilerParams(vmem_limit_bytes=12 * MB)


def on_device(queries, keys, values, log_decay, gain):
    core = lax.axis_index("c")
    keys, values = (pltpu.with_memory_space_constraint(a, pltpu.HBM) for a in (keys, values))
    which = core.astype(jnp.int32).reshape(1)
    heads = log_decay.shape[0]
    chips = HALF * 4

    def own(i, c):
        return c[0] * (HALF // HB) + i

    def other(i, c):
        return (1 - c[0]) * (HALF // HB) + i

    def per_half(kernel, group, ins, outs, shapes, **kw):
        return pl.pallas_call(
            kernel,
            grid_spec=pltpu.PrefetchScalarGridSpec(
                num_scalar_prefetch=1,
                grid=(HALF // HB,),
                in_specs=[s(group) for s in ins],
                out_specs=[s(group) for s in outs],
            ),
            out_shape=shapes,
            compiler_params=params(),
            **kw,
        )

    def tokens(group):
        return pl.BlockSpec((T, HB * W), lambda i, c: (0, group(i, c)))

    def decays(group):
        return pl.BlockSpec((HB, T), lambda i, c: (group(i, c), 0))

    def gains(group):
        return pl.BlockSpec((1, HB * W), lambda i, c: (0, group(i, c)))

    def states(group):
        return pl.BlockSpec((HB, W, W), lambda i, c: (i, 0, 0))

    def small(group):
        return pl.BlockSpec((HB, W), lambda i, c: (i, 0))

    def whole(group):
        return pl.BlockSpec((HALF * W + SPLIT, W), lambda i, c: (0, 0))

    swap = functools.partial(lax.ppermute, axis_name="c", perm=[(0, 1), (1, 0)])
    sent_shape = jax.ShapeDtypeStruct((HALF * W + SPLIT, W), BF)
    [sent] = per_half(
        send_states, other, [decays, tokens, tokens], [whole], [sent_shape],
        cost_estimate=cost(1 << 27, 3 * MB),
    )(which, log_decay, keys, values)
    recv = swap(sent)
    state, decay = per_half(
        own_states, own, [decays, tokens, tokens], [states, small],
        [jax.ShapeDtypeStruct((HALF, W, W), F32), jax.ShapeDtypeStruct((HALF, W), F32)],
        cost_estimate=cost(1 << 27, 3 * MB),
    )(which, log_decay, keys, values)
    smem = pl.BlockSpec(memory_space=pltpu.SMEM)
    vmem = pl.BlockSpec(memory_space=pltpu.VMEM)
    chunks = pl.pallas_call(
        combine,
        in_specs=[smem, vmem, vmem, vmem],
        out_specs=vmem,
        out_shape=jax.ShapeDtypeStruct((chips, ROWS, W), BF),
        compiler_params=params(),
    )(which, state, decay, recv)
    chunks, queries = lax.optimization_barrier((chunks, queries))
    owned = lax.all_to_all(chunks, CHIPS, split_axis=0, concat_axis=0, tiled=True)
    inner = pl.pallas_call(
        within,
        grid=(heads // HB,),
        in_specs=[pl.BlockSpec((HB, T), lambda i: (i, 0))]
        + [pl.BlockSpec((T, HB * W), lambda i: (0, i))] * 3,
        out_specs=pl.BlockSpec((T, HB * W), lambda i: (0, i)),
        out_shape=pltpu.HBM((T, heads * W), F32),
        compiler_params=params(),
        cost_estimate=cost(1 << 31, 10 * MB),
    )(log_decay, queries, keys, values)
    owned, inner = lax.optimization_barrier((owned, inner))
    before = pl.pallas_call(
        scan_chips,
        in_specs=[vmem],
        out_specs=vmem,
        out_shape=jax.ShapeDtypeStruct((chips, 32, W), BF),
        compiler_params=params(),
    )(owned)
    back = lax.all_to_all(before, CHIPS, split_axis=0, concat_axis=0, tiled=True)
    keep, give = pl.pallas_call(
        spread_back,
        in_specs=[smem, vmem, vmem, vmem, vmem],
        out_specs=[vmem, vmem],
        out_shape=[jax.ShapeDtypeStruct((HALF, W, W), BF)] * 2,
        compiler_params=params(),
    )(which, back, state, decay, recv)
    taken = swap(give)
    gain_row = gain.reshape(1, heads * W)
    out_shape = jax.ShapeDtypeStruct((T, heads * W), BF)
    [first] = per_half(
        finish_own, own, [decays, tokens, tokens, states, gains], [tokens], [out_shape],
        cost_estimate=cost(1 << 27, 5 * MB),
    )(which, log_decay, queries, inner, keep, gain_row)

    def left_alone(group):
        return pl.BlockSpec(memory_space=pl.ANY)

    [out] = per_half(
        finish_other, other, [left_alone, decays, tokens, tokens, states, gains], [tokens], [out_shape],
        input_output_aliases={1: 0},
        cost_estimate=cost(1 << 27, 5 * MB),
    )(which, first, log_decay, queries, inner, taken, gain_row)
    return out


def solution(mesh):
    chips = Mesh(mesh.devices.reshape(4, 4, 4, 2), ALL)
    placed = (P(ALL, None), P(ALL, None), P(ALL, None), P(None, ALL), P())
    return jax.shard_map(on_device, mesh=chips, in_specs=placed, out_specs=P(ALL, None), check_vma=False)
```

```python
import functools

import jax
import jax.numpy as jnp
from jax import lax
from jax.experimental import pallas as pl
from jax.experimental.pallas import tpu as pltpu
from jax.sharding import Mesh
from jax.sharding import PartitionSpec as P

BF = jnp.bfloat16
F32 = jnp.float32
CHIPS = ("z", "y", "x")
ALL = ("z", "y", "x", "c")
HB = 8
W = 128
T = 256
HALF = 16
SPLIT = 48
ROWS = 40
PART = 4
MB = 1 << 20
LIMIT = 12
FINISH = 20


def running(x):
    lane = lax.broadcasted_iota(jnp.int32, x.shape, 1)
    step = 1
    while step < x.shape[1]:
        x = x + jnp.where(lane >= step, pltpu.roll(x, step, axis=1), 0.0)
        step *= 2
    return x


def split3(x):
    hi = x.astype(BF).astype(F32)
    mid = (x - hi).astype(BF).astype(F32)
    return hi, mid, x - hi - mid


def dot(a, b, dims=((1,), (0,))):
    return lax.dot_general(a, b, (dims, ((), ())), preferred_element_type=F32)


def load(core_ref, refs, bufs, sem, own):
    half = core_ref[0] if own else 1 - core_ref[0]
    columns = pl.ds(pl.multiple_of(half * HALF * W, HALF * W), HALF * W)
    rows = pl.ds(pl.multiple_of(half * HALF, HALF), HALF)
    views = [r.at[:, columns] for r in refs[:-1]] + [refs[-1].at[rows, :]]
    copies = [pltpu.make_async_copy(v, b, sem.at[n]) for n, (v, b) in enumerate(zip(views, bufs))]
    for c in reversed(copies):
        c.start()
    return copies


def states_of(core_ref, k_ref, v_ref, ld_ref, kbuf, vbuf, dbuf, sem, own, put):
    k_in, v_in, d_in = load(core_ref, (k_ref, v_ref, ld_ref), (kbuf, vbuf, dbuf), sem, own)
    d_in.wait()
    cum = running(dbuf[...])
    total = cum[:, T - 1 :]
    factor = jnp.exp(total - cum)
    k_in.wait()

    def decayed(j):
        kt = kbuf[:, j * W : (j + 1) * W].T
        return (kt.astype(F32) * factor[j : j + 1, :]).astype(BF)

    ready = [decayed(0), decayed(1)]
    v_in.wait()
    for j in range(HALF):
        if j + 2 < HALF:
            ready.append(decayed(j + 2))
        put(j, dot(ready[j], vbuf[:, j * W : (j + 1) * W]))
    return jnp.broadcast_to(jnp.exp(total), (HALF, W))


def send_states(core_ref, k_ref, v_ref, ld_ref, out_ref, *scratch):
    def put(j, state):
        out_ref[j * W : (j + 1) * W, :] = state.astype(BF)

    decay = states_of(core_ref, k_ref, v_ref, ld_ref, *scratch, own=False, put=put)
    first = HALF * W
    for n, term in enumerate(split3(decay)):
        out_ref[first + n * HALF : first + (n + 1) * HALF, :] = term.astype(BF)


def own_states(core_ref, k_ref, v_ref, ld_ref, out_ref, decay_ref, *scratch):
    def put(j, state):
        out_ref[j] = state

    decay_ref[...] = states_of(core_ref, k_ref, v_ref, ld_ref, *scratch, own=True, put=put)


def other_decay(recv_ref):
    first = HALF * W
    terms = [recv_ref[first + n * HALF : first + (n + 1) * HALF, :].astype(F32) for n in range(3)]
    return terms[0] + terms[1] + terms[2]


def combine(core_ref, own_ref, decay_ref, recv_ref, out_ref, first_ref, first_decay_ref):
    here = decay_ref[...]
    there = other_decay(recv_ref)
    earlier = core_ref[0] == 0
    one = jnp.ones_like(here)
    a_own = jnp.where(earlier, there, one)
    a_recv = jnp.where(earlier, one, here)
    first_decay_ref[...] = jnp.where(earlier, here, there)
    terms = split3(here * there)
    zeros = jnp.zeros((ROWS - 32 - 3, W), F32)
    for h in range(HALF):
        tail = jnp.concatenate([t[h : h + 1] for t in terms] + [zeros], axis=0)
        for r in range(4):
            rows = slice(r * 32, (r + 1) * 32)
            own = own_ref[h, rows, :]
            recv = recv_ref[h * W + r * 32 : h * W + (r + 1) * 32, :].astype(F32)
            body = a_own[h : h + 1] * own + a_recv[h : h + 1] * recv
            out_ref[4 * h + r] = jnp.concatenate([body, tail], axis=0).astype(BF)
            first_ref[h, rows, :] = jnp.where(earlier, own, recv).astype(BF)


def scan_chips(in_ref, out_ref):
    carry = jnp.zeros((32, W), F32)
    for j in range(in_ref.shape[0]):
        out_ref[j] = carry.astype(BF)
        x = in_ref[j].astype(F32)
        decay = x[32:33] + x[33:34] + x[34:35]
        carry = decay * carry + x[:32]


def spread_back(core_ref, chip_ref, first_ref, first_decay_ref, keep_ref, send_ref):
    earlier = core_ref[0] == 0
    decay = first_decay_ref[...]
    for h in range(HALF):
        for r in range(4):
            rows = slice(r * 32, (r + 1) * 32)
            first = chip_ref[4 * h + r].astype(F32)
            second = decay[h : h + 1] * first + first_ref[h, rows, :].astype(F32)
            keep_ref[h, rows, :] = jnp.where(earlier, first, second).astype(BF)
            send_ref[h, rows, :] = jnp.where(earlier, second, first).astype(BF)


def within(ld_ref, q_ref, k_ref, v_ref, out_ref):
    cum = running(ld_ref[...])
    cols = cum.T
    n = W
    causal = lax.broadcasted_iota(jnp.int32, (n, n), 0) >= lax.broadcasted_iota(jnp.int32, (n, n), 1)

    def scores(j):
        at = slice(j * W, (j + 1) * W)
        nt = ((1,), (1,))
        return dot(q_ref[:n, at], k_ref[:n, at], nt), dot(q_ref[n:, at], k_ref[:, at], nt)

    def weights(j, upper, lower):
        row, col = cum[j : j + 1, :], cols[:, j : j + 1]

        def decay(t, s):
            gap = col[t * n : (t + 1) * n] - row[:, s * n : (s + 1) * n]
            if t == s:
                gap = jnp.where(causal, gap, -1e30)
            return jnp.exp(jnp.minimum(gap, 0.0))

        low = [lower[:, :n] * decay(1, 0), lower[:, n:] * decay(1, 1)]
        return (upper * decay(0, 0)).astype(BF), jnp.concatenate(low, axis=1).astype(BF)

    def total(j, upper, lower):
        at = slice(j * W, (j + 1) * W)
        out_ref[:n, at] = dot(upper, v_ref[:n, at])
        out_ref[n:, at] = dot(lower, v_ref[:, at])

    following = scores(0)
    waiting = None
    for j in range(HB):
        current = following
        if j + 1 < HB:
            following = scores(j + 1)
        made = weights(j, *current)
        if waiting is not None:
            total(j - 1, *waiting)
        waiting = made
    total(HB - 1, *waiting)


def within_half(core_ref, *refs):
    within(*refs)


def finish_half(core_ref, ld_ref, q_ref, inner_ref, carried_ref, gain_ref, out_ref, buf, sem, own, arrive):
    half = core_ref[0] if own else 1 - core_ref[0]
    grown = jnp.exp(running(ld_ref[pl.ds(pl.multiple_of(half * HALF, HALF), HALF), :])).T
    ones = jnp.full((W, W), 1.0 / W, BF)

    def columns(j, count=1):
        return pl.ds(pl.multiple_of(half * HALF * W + j * W, W), count * W)

    def readout(j):
        return dot(q_ref[:, columns(j)], carried_ref[j])

    copies = []
    following = readout(0)
    for j in range(HALF):
        current = following
        if j + 1 < HALF:
            following = readout(j + 1)
        arrive(j)
        numer = inner_ref[:, j * W : (j + 1) * W] + current * grown[:, j : j + 1]
        mean = dot((numer * numer).astype(BF), ones)
        buf[:, j * W : (j + 1) * W] = (numer * lax.rsqrt(mean + 1e-6) * gain_ref[:, columns(j)]).astype(BF)
        if j % PART == PART - 1:
            at = j + 1 - PART
            copy = pltpu.make_async_copy(
                buf.at[:, at * W : (j + 1) * W], out_ref.at[:, columns(at, PART)], sem.at[j // PART]
            )
            copy.start()
            copies.append(copy)
    for copy in copies:
        copy.wait()


def finish_own(core_ref, ld_ref, q_ref, far_inner, carried_ref, gain_ref, out_ref, buf, sem, inner, arrived):
    parts = []
    for p in range(HALF // PART):
        at = slice(p * PART * W, (p + 1) * PART * W)
        parts.append(pltpu.make_async_copy(far_inner.at[:, at], inner.at[:, at], arrived.at[p]))
        parts[p].start()

    def arrive(j):
        if j % PART == 0:
            parts[j // PART].wait()

    finish_half(core_ref, ld_ref, q_ref, inner, carried_ref, gain_ref, out_ref, buf, sem, True, arrive)


def finish_other(core_ref, old_ref, *refs):
    finish_half(core_ref, *refs, False, lambda j: None)


def cost(flops, bytes_accessed):
    return pl.CostEstimate(flops=flops, bytes_accessed=bytes_accessed, transcendentals=0)


def call(kernel, ins, outs, shapes, scratch=(), limit=LIMIT, **kw):
    return pl.pallas_call(
        kernel,
        in_specs=ins,
        out_specs=outs,
        out_shape=shapes,
        scratch_shapes=list(scratch),
        compiler_params=pltpu.CompilerParams(vmem_limit_bytes=limit * MB),
        **kw,
    )


def block_half(kernel, own, which, arrays):
    def group(i, core):
        return (core[0] if own else 1 - core[0]) * (HALF // HB) + i

    return pl.pallas_call(
        kernel,
        grid_spec=pltpu.PrefetchScalarGridSpec(
            num_scalar_prefetch=1,
            grid=(HALF // HB,),
            in_specs=[pl.BlockSpec((HB, T), lambda i, c: (group(i, c), 0))]
            + [pl.BlockSpec((T, HB * W), lambda i, c: (0, group(i, c)))] * 3,
            out_specs=pl.BlockSpec((T, HB * W), lambda i, c: (0, i)),
        ),
        out_shape=pltpu.HBM((T, HALF * W), F32),
        compiler_params=pltpu.CompilerParams(vmem_limit_bytes=LIMIT * MB),
        cost_estimate=cost(1 << 30, 5 * MB),
    )(which, *arrays)


def on_device(queries, keys, values, log_decay, gain):
    which = lax.axis_index("c").astype(jnp.int32).reshape(1)
    heads = log_decay.shape[0]
    chips = HALF * 4
    smem = pl.BlockSpec(memory_space=pltpu.SMEM)
    vmem = pl.BlockSpec(memory_space=pltpu.VMEM)
    hbm = pl.BlockSpec(memory_space=pltpu.HBM)
    struct = jax.ShapeDtypeStruct
    far_q, far_k, far_v, far_ld = (
        pltpu.with_memory_space_constraint(a, pltpu.HBM) for a in (queries, keys, values, log_decay)
    )
    swap = functools.partial(lax.ppermute, axis_name="c", perm=[(0, 1), (1, 0)])
    halves = [
        pltpu.VMEM((T, HALF * W), BF),
        pltpu.VMEM((T, HALF * W), BF),
        pltpu.VMEM((HALF, T), F32),
        pltpu.SemaphoreType.DMA((3,)),
    ]
    sources = (which, far_k, far_v, far_ld)
    sent = call(
        send_states, [smem, hbm, hbm, hbm], vmem, struct((HALF * W + SPLIT, W), BF), halves,
        cost_estimate=cost(1 << 27, 3 * MB),
    )(*sources)
    recv = swap(sent)
    state, decay = call(
        own_states, [smem, hbm, hbm, hbm], [vmem, vmem],
        [struct((HALF, W, W), F32), struct((HALF, W), F32)], halves,
        cost_estimate=cost(1 << 27, 3 * MB),
    )(*sources)
    chunks, first, first_decay = call(
        combine, [smem, vmem, vmem, vmem], [vmem] * 3,
        [struct((chips, ROWS, W), BF), struct((HALF, W, W), BF), struct((HALF, W), F32)],
    )(which, state, decay, recv)
    chunks, far_q = lax.optimization_barrier((chunks, far_q))
    owned = lax.all_to_all(chunks, CHIPS, split_axis=0, concat_axis=0, tiled=True)
    near = block_half(within_half, True, which, (far_ld, far_q, far_k, far_v))
    far = block_half(within_half, False, which, (far_ld, far_q, far_k, far_v))
    owned, near, far = lax.optimization_barrier((owned, near, far))
    before = call(scan_chips, [vmem], vmem, struct((chips, 32, W), BF))(owned)
    back = lax.all_to_all(before, CHIPS, split_axis=0, concat_axis=0, tiled=True)
    keep, give = call(
        spread_back, [smem, vmem, vmem, vmem], [vmem] * 2, [struct((HALF, W, W), BF)] * 2
    )(which, back, first, first_decay)
    taken = swap(give)
    late = (log_decay, queries)
    gains = gain.reshape(1, heads * W)
    out_shape = pltpu.HBM((T, heads * W), BF)
    bufs = [pltpu.VMEM((T, HALF * W), BF), pltpu.SemaphoreType.DMA((HALF // PART,))]
    inner_bufs = [pltpu.VMEM((T, HALF * W), F32), pltpu.SemaphoreType.DMA((HALF // PART,))]
    started = call(
        finish_own, [smem, vmem, vmem, hbm, vmem, vmem], hbm, out_shape, bufs + inner_bufs, FINISH, cost_estimate=cost(1 << 27, 5 * MB)
    )(which, *late, near, keep, gains)
    return call(
        finish_other, [smem, hbm] + [vmem] * 5, hbm, out_shape, bufs, FINISH,
        input_output_aliases={1: 0}, cost_estimate=cost(1 << 27, 5 * MB),
    )(which, started, *late, far, taken, gains)


def solution(mesh):
    chips = Mesh(mesh.devices.reshape(4, 4, 4, 2), ALL)
    placed = (P(ALL, None), P(ALL, None), P(ALL, None), P(None, ALL), P())
    return jax.shard_map(on_device, mesh=chips, in_specs=placed, out_specs=P(ALL, None), check_vma=False)
```

```python
import functools

import jax
import jax.numpy as jnp
from jax import lax
from jax.experimental import pallas as pl
from jax.experimental.pallas import tpu as pltpu
from jax.sharding import Mesh
from jax.sharding import PartitionSpec as P

BF = jnp.bfloat16
F32 = jnp.float32
CHIPS = ("z", "y", "x")
ALL = ("z", "y", "x", "c")
HB = 8
W = 128
T = 256
HALF = 16
SPLIT = 48
ROWS = 40
AHEAD = 1
PART = 4
MB = 1 << 20
LIMIT = 12
FINISH = 20


def running(x):
    lane = lax.broadcasted_iota(jnp.int32, x.shape, 1)
    step = 1
    while step < x.shape[1]:
        x = x + jnp.where(lane >= step, pltpu.roll(x, step, axis=1), 0.0)
        step *= 2
    return x


def split3(x):
    hi = x.astype(BF).astype(F32)
    mid = (x - hi).astype(BF).astype(F32)
    return hi, mid, x - hi - mid


def dot(a, b, dims=((1,), (0,))):
    return lax.dot_general(a, b, (dims, ((), ())), preferred_element_type=F32)


def load(core_ref, refs, bufs, sem, own):
    half = core_ref[0] if own else 1 - core_ref[0]
    columns = pl.ds(pl.multiple_of(half * HALF * W, HALF * W), HALF * W)
    rows = pl.ds(pl.multiple_of(half * HALF, HALF), HALF)
    views = [r.at[:, columns] for r in refs[:-1]] + [refs[-1].at[rows, :]]
    copies = [pltpu.make_async_copy(v, b, sem.at[n]) for n, (v, b) in enumerate(zip(views, bufs))]
    for c in reversed(copies):
        c.start()
    return copies


def states_of(core_ref, k_ref, v_ref, ld_ref, kbuf, vbuf, dbuf, sem, own, put):
    k_in, v_in, d_in = load(core_ref, (k_ref, v_ref, ld_ref), (kbuf, vbuf, dbuf), sem, own)
    d_in.wait()
    cum = running(dbuf[...])
    total = cum[:, T - 1 :]
    factor = jnp.exp(total - cum)
    k_in.wait()

    def decayed(j):
        kt = kbuf[:, j * W : (j + 1) * W].T
        return (kt.astype(F32) * factor[j : j + 1, :]).astype(BF)

    ready = [decayed(0), decayed(1)]
    v_in.wait()
    for j in range(HALF):
        if j + 2 < HALF:
            ready.append(decayed(j + 2))
        put(j, dot(ready[j], vbuf[:, j * W : (j + 1) * W]))
    return jnp.broadcast_to(jnp.exp(total), (HALF, W))


def send_states(core_ref, k_ref, v_ref, ld_ref, out_ref, *scratch):
    def put(j, state):
        out_ref[j * W : (j + 1) * W, :] = state.astype(BF)

    decay = states_of(core_ref, k_ref, v_ref, ld_ref, *scratch, own=False, put=put)
    first = HALF * W
    for n, term in enumerate(split3(decay)):
        out_ref[first + n * HALF : first + (n + 1) * HALF, :] = term.astype(BF)


def own_states(core_ref, k_ref, v_ref, ld_ref, out_ref, decay_ref, *scratch):
    def put(j, state):
        out_ref[j] = state

    decay_ref[...] = states_of(core_ref, k_ref, v_ref, ld_ref, *scratch, own=True, put=put)


def other_decay(recv_ref):
    first = HALF * W
    terms = [recv_ref[first + n * HALF : first + (n + 1) * HALF, :].astype(F32) for n in range(3)]
    return terms[0] + terms[1] + terms[2]


def combine(core_ref, own_ref, decay_ref, recv_ref, out_ref, first_ref, first_decay_ref):
    here = decay_ref[...]
    there = other_decay(recv_ref)
    earlier = core_ref[0] == 0
    one = jnp.ones_like(here)
    a_own = jnp.where(earlier, there, one)
    a_recv = jnp.where(earlier, one, here)
    first_decay_ref[...] = jnp.where(earlier, here, there)
    terms = split3(here * there)
    zeros = jnp.zeros((ROWS - 32 - 3, W), F32)
    for h in range(HALF):
        tail = jnp.concatenate([t[h : h + 1] for t in terms] + [zeros], axis=0)
        for r in range(4):
            rows = slice(r * 32, (r + 1) * 32)
            own = own_ref[h, rows, :]
            recv = recv_ref[h * W + r * 32 : h * W + (r + 1) * 32, :].astype(F32)
            body = a_own[h : h + 1] * own + a_recv[h : h + 1] * recv
            out_ref[4 * h + r] = jnp.concatenate([body, tail], axis=0).astype(BF)
            first_ref[h, rows, :] = jnp.where(earlier, own, recv).astype(BF)


def scan_chips(in_ref, out_ref):
    carry = jnp.zeros((32, W), F32)
    for j in range(in_ref.shape[0]):
        out_ref[j] = carry.astype(BF)
        x = in_ref[j].astype(F32)
        decay = x[32:33] + x[33:34] + x[34:35]
        carry = decay * carry + x[:32]


def spread_back(core_ref, chip_ref, first_ref, first_decay_ref, keep_ref, send_ref):
    earlier = core_ref[0] == 0
    decay = first_decay_ref[...]
    for h in range(HALF):
        for r in range(4):
            rows = slice(r * 32, (r + 1) * 32)
            first = chip_ref[4 * h + r].astype(F32)
            second = decay[h : h + 1] * first + first_ref[h, rows, :].astype(F32)
            keep_ref[h, rows, :] = jnp.where(earlier, first, second).astype(BF)
            send_ref[h, rows, :] = jnp.where(earlier, second, first).astype(BF)


def within(core_ref, ld_ref, q_ref, k_ref, v_ref, out_ref):
    cum = running(ld_ref[...])
    cols = cum.T
    n = W
    causal = lax.broadcasted_iota(jnp.int32, (n, n), 0) >= lax.broadcasted_iota(jnp.int32, (n, n), 1)

    def scores(j):
        at = slice(j * W, (j + 1) * W)
        nt = ((1,), (1,))
        return dot(q_ref[:n, at], k_ref[:n, at], nt), dot(q_ref[n:, at], k_ref[:, at], nt)

    def weights(j, upper, lower):
        row, col = cum[j : j + 1, :], cols[:, j : j + 1]

        def decay(t, s):
            gap = col[t * n : (t + 1) * n] - row[:, s * n : (s + 1) * n]
            if t == s:
                gap = jnp.where(causal, gap, -1e30)
            return jnp.exp(jnp.minimum(gap, 0.0))

        low = [lower[:, :n] * decay(1, 0), lower[:, n:] * decay(1, 1)]
        return (upper * decay(0, 0)).astype(BF), jnp.concatenate(low, axis=1).astype(BF)

    def total(j, upper, lower):
        at = slice(j * W, (j + 1) * W)
        out_ref[:n, at] = dot(upper, v_ref[:n, at])
        out_ref[n:, at] = dot(lower, v_ref[:, at])

    following = scores(0)
    waiting = None
    for j in range(HB):
        current = following
        if j + 1 < HB:
            following = scores(j + 1)
        made = weights(j, *current)
        if waiting is not None:
            total(j - 1, *waiting)
        waiting = made
    total(HB - 1, *waiting)


def finish_half(half, ld_ref, q_ref, inner_ref, carried_ref, gain_ref, put, arrive, skip):
    grown = jnp.exp(running(ld_ref[pl.ds(pl.multiple_of(half * HALF, HALF), HALF), :])).T
    ones = jnp.full((W, W), 1.0 / W, BF)

    def columns(j):
        return pl.ds(pl.multiple_of(half * HALF * W + j * W, W), W)

    def readout(j):
        return dot(q_ref[:, columns(j)], carried_ref[j])

    ready = [readout(j) for j in range(AHEAD)]
    for j in range(HALF):
        if j + AHEAD < HALF:
            ready.append(readout(j + AHEAD))
        arrive(j)
        at = slice((skip + j) * W, (skip + j + 1) * W)
        numer = inner_ref[:, at] + ready[j] * grown[:, j : j + 1]
        mean = dot((numer * numer).astype(BF), ones)
        put(j, (numer * lax.rsqrt(mean + 1e-6) * gain_ref[:, columns(j)]).astype(BF))


def finish_own(core_ref, ld_ref, q_ref, far_inner, carried_ref, gain_ref, out_ref, inner, arrived):
    parts = []
    for p in range(HALF // PART):
        at = slice(p * PART * W, (p + 1) * PART * W)
        parts.append(pltpu.make_async_copy(far_inner.at[:, at], inner.at[:, at], arrived.at[p]))
        parts[p].start()

    def arrive(j):
        if j % PART == 0:
            parts[j // PART].wait()

    def put(j, value):
        out_ref[:, j * W : (j + 1) * W] = value

    finish_half(core_ref[0], ld_ref, q_ref, inner, carried_ref, gain_ref, put, arrive, 0)


def finish_other(core_ref, own_ref, ld_ref, q_ref, inner_ref, carried_ref, gain_ref, out_ref, buf, sem):
    half = 1 - core_ref[0]
    first = pl.ds(pl.multiple_of(core_ref[0] * HALF * W, HALF * W), HALF * W)
    copies = [pltpu.make_async_copy(own_ref, out_ref.at[:, first], sem.at[HALF // PART])]
    copies[0].start()

    def put(j, value):
        buf[:, j * W : (j + 1) * W] = value
        if j % PART == PART - 1:
            at = j + 1 - PART
            to = pl.ds(pl.multiple_of(half * HALF * W + at * W, W), PART * W)
            copy = pltpu.make_async_copy(buf.at[:, at * W : (j + 1) * W], out_ref.at[:, to], sem.at[j // PART])
            copy.start()
            copies.append(copy)

    finish_half(half, ld_ref, q_ref, inner_ref, carried_ref, gain_ref, put, lambda j: None, HALF)
    for copy in copies:
        copy.wait()


def cost(flops, bytes_accessed):
    return pl.CostEstimate(flops=flops, bytes_accessed=bytes_accessed, transcendentals=0)


def call(kernel, ins, outs, shapes, scratch=(), limit=LIMIT, **kw):
    return pl.pallas_call(
        kernel,
        in_specs=ins,
        out_specs=outs,
        out_shape=shapes,
        scratch_shapes=list(scratch),
        compiler_params=pltpu.CompilerParams(vmem_limit_bytes=limit * MB),
        **kw,
    )


def within_blocks(which, *arrays):
    groups = 2 * HALF // HB

    def group(i, core):
        return (core[0] * (HALF // HB) + i) % groups

    return pl.pallas_call(
        within,
        grid_spec=pltpu.PrefetchScalarGridSpec(
            num_scalar_prefetch=1,
            grid=(groups,),
            in_specs=[pl.BlockSpec((HB, T), lambda i, c: (group(i, c), 0))]
            + [pl.BlockSpec((T, HB * W), lambda i, c: (0, group(i, c)))] * 3,
            out_specs=pl.BlockSpec((T, HB * W), lambda i, c: (0, i)),
        ),
        out_shape=pltpu.HBM((T, groups * HB * W), F32),
        compiler_params=pltpu.CompilerParams(vmem_limit_bytes=LIMIT * MB),
        cost_estimate=cost(1 << 31, 10 * MB),
    )(which, *arrays)


def on_device(queries, keys, values, log_decay, gain):
    which = lax.axis_index("c").astype(jnp.int32).reshape(1)
    heads = log_decay.shape[0]
    chips = HALF * 4
    smem = pl.BlockSpec(memory_space=pltpu.SMEM)
    vmem = pl.BlockSpec(memory_space=pltpu.VMEM)
    hbm = pl.BlockSpec(memory_space=pltpu.HBM)
    struct = jax.ShapeDtypeStruct
    far_q, far_k, far_v, far_ld = (
        pltpu.with_memory_space_constraint(a, pltpu.HBM) for a in (queries, keys, values, log_decay)
    )
    swap = functools.partial(lax.ppermute, axis_name="c", perm=[(0, 1), (1, 0)])
    halves = [
        pltpu.VMEM((T, HALF * W), BF),
        pltpu.VMEM((T, HALF * W), BF),
        pltpu.VMEM((HALF, T), F32),
        pltpu.SemaphoreType.DMA((3,)),
    ]
    sources = (which, far_k, far_v, far_ld)
    sent = call(
        send_states, [smem, hbm, hbm, hbm], vmem, struct((HALF * W + SPLIT, W), BF), halves,
        cost_estimate=cost(1 << 27, 3 * MB),
    )(*sources)
    recv = swap(sent)
    state, decay = call(
        own_states, [smem, hbm, hbm, hbm], [vmem, vmem],
        [struct((HALF, W, W), F32), struct((HALF, W), F32)], halves,
        cost_estimate=cost(1 << 27, 3 * MB),
    )(*sources)
    chunks, first, first_decay = call(
        combine, [smem, vmem, vmem, vmem], [vmem] * 3,
        [struct((chips, ROWS, W), BF), struct((HALF, W, W), BF), struct((HALF, W), F32)],
    )(which, state, decay, recv)
    chunks, far_q = lax.optimization_barrier((chunks, far_q))
    owned = lax.all_to_all(chunks, CHIPS, split_axis=0, concat_axis=0, tiled=True)
    inner = within_blocks(which, far_ld, far_q, far_k, far_v)
    owned, inner = lax.optimization_barrier((owned, inner))
    before = call(scan_chips, [vmem], vmem, struct((chips, 32, W), BF))(owned)
    back = lax.all_to_all(before, CHIPS, split_axis=0, concat_axis=0, tiled=True)
    keep, give = call(
        spread_back, [smem, vmem, vmem, vmem], [vmem] * 2, [struct((HALF, W, W), BF)] * 2
    )(which, back, first, first_decay)
    taken = swap(give)
    gains = gain.reshape(1, heads * W)
    started = call(
        finish_own, [smem, vmem, vmem, hbm, vmem, vmem], vmem, struct((T, HALF * W), BF),
        [pltpu.VMEM((T, HALF * W), F32), pltpu.SemaphoreType.DMA((HALF // PART,))], FINISH,
        cost_estimate=cost(1 << 27, 5 * MB),
    )(which, log_decay, queries, pltpu.with_memory_space_constraint(inner, pltpu.HBM), keep, gains)
    return call(
        finish_other, [smem] + [vmem] * 6, hbm, pltpu.HBM((T, heads * W), BF),
        [pltpu.VMEM((T, HALF * W), BF), pltpu.SemaphoreType.DMA((HALF // PART + 1,))], FINISH,
        cost_estimate=cost(1 << 27, 5 * MB),
    )(which, started, log_decay, queries, inner, taken, gains)


def solution(mesh):
    chips = Mesh(mesh.devices.reshape(4, 4, 4, 2), ALL)
    placed = (P(ALL, None), P(ALL, None), P(ALL, None), P(None, ALL), P())
    return jax.shard_map(on_device, mesh=chips, in_specs=placed, out_specs=P(ALL, None), check_vma=False)
```

```python
import functools

import jax
import jax.numpy as jnp
from jax import lax
from jax.experimental import pallas as pl
from jax.experimental.pallas import tpu as pltpu
from jax.sharding import Mesh
from jax.sharding import PartitionSpec as P

BF = jnp.bfloat16
F32 = jnp.float32
CHIPS = ("z", "y", "x")
ALL = ("z", "y", "x", "c")
HB = 8
W = 128
T = 256
HALF = 16
SPLIT = 48
ROWS = 40
AHEAD = 1
PART = 4
MB = 1 << 20
LIMIT = 12
FINISH = 20


def running(x):
    lane = lax.broadcasted_iota(jnp.int32, x.shape, 1)
    step = 1
    while step < x.shape[1]:
        x = x + jnp.where(lane >= step, pltpu.roll(x, step, axis=1), 0.0)
        step *= 2
    return x


def split3(x):
    hi = x.astype(BF).astype(F32)
    mid = (x - hi).astype(BF).astype(F32)
    return hi, mid, x - hi - mid


def dot(a, b, dims=((1,), (0,))):
    return lax.dot_general(a, b, (dims, ((), ())), preferred_element_type=F32)


def load(core_ref, refs, bufs, sem, own):
    half = core_ref[0] if own else 1 - core_ref[0]
    columns = pl.ds(pl.multiple_of(half * HALF * W, HALF * W), HALF * W)
    rows = pl.ds(pl.multiple_of(half * HALF, HALF), HALF)
    views = [r.at[:, columns] for r in refs[:-1]] + [refs[-1].at[rows, :]]
    copies = [pltpu.make_async_copy(v, b, sem.at[n]) for n, (v, b) in enumerate(zip(views, bufs))]
    for c in reversed(copies):
        c.start()
    return copies


def states_of(core_ref, k_ref, v_ref, ld_ref, kbuf, vbuf, dbuf, sem, own, put):
    k_in, v_in, d_in = load(core_ref, (k_ref, v_ref, ld_ref), (kbuf, vbuf, dbuf), sem, own)
    d_in.wait()
    cum = running(dbuf[...])
    total = cum[:, T - 1 :]
    factor = jnp.exp(total - cum)
    k_in.wait()

    def decayed(j):
        kt = kbuf[:, j * W : (j + 1) * W].T
        return (kt.astype(F32) * factor[j : j + 1, :]).astype(BF)

    ready = [decayed(0), decayed(1)]
    v_in.wait()
    for j in range(HALF):
        if j + 2 < HALF:
            ready.append(decayed(j + 2))
        put(j, dot(ready[j], vbuf[:, j * W : (j + 1) * W]))
    return jnp.broadcast_to(jnp.exp(total), (HALF, W))


def send_states(core_ref, k_ref, v_ref, ld_ref, out_ref, *scratch):
    def put(j, state):
        out_ref[j * W : (j + 1) * W, :] = state.astype(BF)

    decay = states_of(core_ref, k_ref, v_ref, ld_ref, *scratch, own=False, put=put)
    first = HALF * W
    for n, term in enumerate(split3(decay)):
        out_ref[first + n * HALF : first + (n + 1) * HALF, :] = term.astype(BF)


def own_states(core_ref, k_ref, v_ref, ld_ref, out_ref, decay_ref, *scratch):
    def put(j, state):
        out_ref[j] = state

    decay_ref[...] = states_of(core_ref, k_ref, v_ref, ld_ref, *scratch, own=True, put=put)


def other_decay(recv_ref):
    first = HALF * W
    terms = [recv_ref[first + n * HALF : first + (n + 1) * HALF, :].astype(F32) for n in range(3)]
    return terms[0] + terms[1] + terms[2]


def combine(core_ref, own_ref, decay_ref, recv_ref, out_ref, first_ref, first_decay_ref):
    here = decay_ref[...]
    there = other_decay(recv_ref)
    earlier = core_ref[0] == 0
    one = jnp.ones_like(here)
    a_own = jnp.where(earlier, there, one)
    a_recv = jnp.where(earlier, one, here)
    first_decay_ref[...] = jnp.where(earlier, here, there)
    terms = split3(here * there)
    zeros = jnp.zeros((ROWS - 32 - 3, W), F32)
    for h in range(HALF):
        tail = jnp.concatenate([t[h : h + 1] for t in terms] + [zeros], axis=0)
        for r in range(4):
            rows = slice(r * 32, (r + 1) * 32)
            own = own_ref[h, rows, :]
            recv = recv_ref[h * W + r * 32 : h * W + (r + 1) * 32, :].astype(F32)
            body = a_own[h : h + 1] * own + a_recv[h : h + 1] * recv
            out_ref[4 * h + r] = jnp.concatenate([body, tail], axis=0).astype(BF)
            first_ref[h, rows, :] = jnp.where(earlier, own, recv).astype(BF)


def scan_chips(in_ref, out_ref):
    carry = jnp.zeros((32, W), F32)
    for j in range(in_ref.shape[0]):
        out_ref[j] = carry.astype(BF)
        x = in_ref[j].astype(F32)
        decay = x[32:33] + x[33:34] + x[34:35]
        carry = decay * carry + x[:32]


def spread_back(core_ref, near_ref, chip_ref, first_ref, first_decay_ref, keep_ref, send_ref):
    earlier = core_ref[0] == 0
    decay = first_decay_ref[...]
    for h in range(HALF):
        for r in range(4):
            rows = slice(r * 32, (r + 1) * 32)
            first = chip_ref[4 * h + r].astype(F32)
            second = decay[h : h + 1] * first + first_ref[h, rows, :].astype(F32)
            keep_ref[h, rows, :] = jnp.where(earlier, first, second).astype(BF)
            send_ref[h, rows, :] = jnp.where(earlier, second, first).astype(BF)


def within(core_ref, ld_ref, q_ref, k_ref, v_ref, near_ref, far_ref):
    @pl.when(pl.program_id(0) < HALF // HB)
    def _():
        within_step(ld_ref, q_ref, k_ref, v_ref, near_ref)

    @pl.when(pl.program_id(0) >= HALF // HB)
    def _():
        within_step(ld_ref, q_ref, k_ref, v_ref, far_ref)


def within_step(ld_ref, q_ref, k_ref, v_ref, out_ref):
    cum = running(ld_ref[...])
    cols = cum.T
    n = W
    causal = lax.broadcasted_iota(jnp.int32, (n, n), 0) >= lax.broadcasted_iota(jnp.int32, (n, n), 1)

    def scores(j):
        at = slice(j * W, (j + 1) * W)
        nt = ((1,), (1,))
        return dot(q_ref[:n, at], k_ref[:n, at], nt), dot(q_ref[n:, at], k_ref[:, at], nt)

    def weights(j, upper, lower):
        row, col = cum[j : j + 1, :], cols[:, j : j + 1]

        def decay(t, s):
            gap = col[t * n : (t + 1) * n] - row[:, s * n : (s + 1) * n]
            if t == s:
                gap = jnp.where(causal, gap, -1e30)
            return jnp.exp(jnp.minimum(gap, 0.0))

        low = [lower[:, :n] * decay(1, 0), lower[:, n:] * decay(1, 1)]
        return (upper * decay(0, 0)).astype(BF), jnp.concatenate(low, axis=1).astype(BF)

    def total(j, upper, lower):
        at = slice(j * W, (j + 1) * W)
        out_ref[:n, at] = dot(upper, v_ref[:n, at])
        out_ref[n:, at] = dot(lower, v_ref[:, at])

    following = scores(0)
    waiting = None
    for j in range(HB):
        current = following
        if j + 1 < HB:
            following = scores(j + 1)
        made = weights(j, *current)
        if waiting is not None:
            total(j - 1, *waiting)
        waiting = made
    total(HB - 1, *waiting)


def finish_half(half, ld_ref, q_ref, inner_ref, carried_ref, gain_ref, put):
    grown = jnp.exp(running(ld_ref[pl.ds(pl.multiple_of(half * HALF, HALF), HALF), :])).T
    ones = jnp.full((W, W), 1.0 / W, BF)

    def columns(j):
        return pl.ds(pl.multiple_of(half * HALF * W + j * W, W), W)

    def readout(j):
        return dot(q_ref[:, columns(j)], carried_ref[j])

    ready = [readout(j) for j in range(AHEAD)]
    for j in range(HALF):
        if j + AHEAD < HALF:
            ready.append(readout(j + AHEAD))
        at = slice(j * W, (j + 1) * W)
        numer = inner_ref[:, at] + ready[j] * grown[:, j : j + 1]
        mean = dot((numer * numer).astype(BF), ones)
        put(j, (numer * lax.rsqrt(mean + 1e-6) * gain_ref[:, columns(j)]).astype(BF))


def finish_own(core_ref, ld_ref, q_ref, inner_ref, carried_ref, gain_ref, out_ref):
    def put(j, value):
        out_ref[:, j * W : (j + 1) * W] = value

    finish_half(core_ref[0], ld_ref, q_ref, inner_ref, carried_ref, gain_ref, put)


def finish_other(core_ref, own_ref, ld_ref, q_ref, inner_ref, carried_ref, gain_ref, out_ref, buf, sem):
    half = 1 - core_ref[0]
    first = pl.ds(pl.multiple_of(core_ref[0] * HALF * W, HALF * W), HALF * W)
    copies = [pltpu.make_async_copy(own_ref, out_ref.at[:, first], sem.at[HALF // PART])]
    copies[0].start()

    def put(j, value):
        buf[:, j * W : (j + 1) * W] = value
        if j % PART == PART - 1:
            at = j + 1 - PART
            to = pl.ds(pl.multiple_of(half * HALF * W + at * W, W), PART * W)
            copy = pltpu.make_async_copy(buf.at[:, at * W : (j + 1) * W], out_ref.at[:, to], sem.at[j // PART])
            copy.start()
            copies.append(copy)

    finish_half(half, ld_ref, q_ref, inner_ref, carried_ref, gain_ref, put)
    for copy in copies:
        copy.wait()


def cost(flops, bytes_accessed):
    return pl.CostEstimate(flops=flops, bytes_accessed=bytes_accessed, transcendentals=0)


def call(kernel, ins, outs, shapes, scratch=(), limit=LIMIT, **kw):
    return pl.pallas_call(
        kernel,
        in_specs=ins,
        out_specs=outs,
        out_shape=shapes,
        scratch_shapes=list(scratch),
        compiler_params=pltpu.CompilerParams(vmem_limit_bytes=limit * MB),
        **kw,
    )


def within_blocks(which, *arrays):
    groups = 2 * HALF // HB

    def group(i, core):
        return (core[0] * (HALF // HB) + i) % groups

    return pl.pallas_call(
        within,
        grid_spec=pltpu.PrefetchScalarGridSpec(
            num_scalar_prefetch=1,
            grid=(groups,),
            in_specs=[pl.BlockSpec((HB, T), lambda i, c: (group(i, c), 0))]
            + [pl.BlockSpec((T, HB * W), lambda i, c: (0, group(i, c)))] * 3,
            out_specs=[
                pl.BlockSpec((T, HB * W), lambda i, c: (0, jnp.minimum(i, groups // 2 - 1))),
                pl.BlockSpec((T, HB * W), lambda i, c: (0, jnp.maximum(i - groups // 2, 0))),
            ],
        ),
        out_shape=[pltpu.HBM((T, HALF * W), F32)] * 2,
        compiler_params=pltpu.CompilerParams(vmem_limit_bytes=LIMIT * MB),
        cost_estimate=cost(1 << 31, 10 * MB),
    )(which, *arrays)


def on_device(queries, keys, values, log_decay, gain):
    which = lax.axis_index("c").astype(jnp.int32).reshape(1)
    heads = log_decay.shape[0]
    chips = HALF * 4
    smem = pl.BlockSpec(memory_space=pltpu.SMEM)
    vmem = pl.BlockSpec(memory_space=pltpu.VMEM)
    hbm = pl.BlockSpec(memory_space=pltpu.HBM)
    struct = jax.ShapeDtypeStruct
    far_q, far_k, far_v, far_ld = (
        pltpu.with_memory_space_constraint(a, pltpu.HBM) for a in (queries, keys, values, log_decay)
    )
    swap = functools.partial(lax.ppermute, axis_name="c", perm=[(0, 1), (1, 0)])
    halves = [
        pltpu.VMEM((T, HALF * W), BF),
        pltpu.VMEM((T, HALF * W), BF),
        pltpu.VMEM((HALF, T), F32),
        pltpu.SemaphoreType.DMA((3,)),
    ]
    sources = (which, far_k, far_v, far_ld)
    sent = call(
        send_states, [smem, hbm, hbm, hbm], vmem, struct((HALF * W + SPLIT, W), BF), halves,
        cost_estimate=cost(1 << 27, 3 * MB),
    )(*sources)
    recv = swap(sent)
    state, decay = call(
        own_states, [smem, hbm, hbm, hbm], [vmem, vmem],
        [struct((HALF, W, W), F32), struct((HALF, W), F32)], halves,
        cost_estimate=cost(1 << 27, 3 * MB),
    )(*sources)
    chunks, first, first_decay = call(
        combine, [smem, vmem, vmem, vmem], [vmem] * 3,
        [struct((chips, ROWS, W), BF), struct((HALF, W, W), BF), struct((HALF, W), F32)],
    )(which, state, decay, recv)
    chunks, far_q = lax.optimization_barrier((chunks, far_q))
    owned = lax.all_to_all(chunks, CHIPS, split_axis=0, concat_axis=0, tiled=True)
    near, far = within_blocks(which, far_ld, far_q, far_k, far_v)
    owned, near, far = lax.optimization_barrier((owned, near, far))
    before = call(scan_chips, [vmem], vmem, struct((chips, 32, W), BF), cost_estimate=cost(1 << 10, 1 << 10))(owned)
    back = lax.all_to_all(before, CHIPS, split_axis=0, concat_axis=0, tiled=True)
    keep, give = call(
        spread_back, [smem, vmem, vmem, vmem, vmem], [vmem] * 2, [struct((HALF, W, W), BF)] * 2,
        cost_estimate=cost(1 << 10, 1 << 10),
    )(which, near, back, first, first_decay)
    taken = swap(give)
    gains = gain.reshape(1, heads * W)
    started = call(
        finish_own, [smem] + [vmem] * 5, vmem, struct((T, HALF * W), BF), limit=FINISH,
        cost_estimate=cost(1 << 27, 5 * MB),
    )(which, log_decay, queries, near, keep, gains)
    return call(
        finish_other, [smem] + [vmem] * 6, hbm, pltpu.HBM((T, heads * W), BF),
        [pltpu.VMEM((T, HALF * W), BF), pltpu.SemaphoreType.DMA((HALF // PART + 1,))], FINISH,
        cost_estimate=cost(1 << 27, 5 * MB),
    )(which, started, log_decay, queries, far, taken, gains)


def solution(mesh):
    chips = Mesh(mesh.devices.reshape(4, 4, 4, 2), ALL)
    placed = (P(ALL, None), P(ALL, None), P(ALL, None), P(None, ALL), P())
    return jax.shard_map(on_device, mesh=chips, in_specs=placed, out_specs=P(ALL, None), check_vma=False)
```

```python
import functools

import jax
import jax.numpy as jnp
from jax import lax
from jax.experimental import pallas as pl
from jax.experimental.pallas import tpu as pltpu
from jax.sharding import Mesh
from jax.sharding import PartitionSpec as P

BF = jnp.bfloat16
F32 = jnp.float32
CHIPS = ("z", "y", "x")
ALL = ("z", "y", "x", "c")
HB = 8
W = 128
T = 256
HALF = 16
SPLIT = 48
ROWS = 40
AHEAD = 1
READY = 4
PART = 4
MB = 1 << 20
LIMIT = 12
FINISH = 20


def running(x):
    lane = lax.broadcasted_iota(jnp.int32, x.shape, 1)
    step = 1
    while step < x.shape[1]:
        x = x + jnp.where(lane >= step, pltpu.roll(x, step, axis=1), 0.0)
        step *= 2
    return x


def split3(x):
    hi = x.astype(BF).astype(F32)
    mid = (x - hi).astype(BF).astype(F32)
    return hi, mid, x - hi - mid


def dot(a, b, dims=((1,), (0,))):
    return lax.dot_general(a, b, (dims, ((), ())), preferred_element_type=F32)


def load(core_ref, refs, bufs, sem, own):
    half = core_ref[0] if own else 1 - core_ref[0]
    columns = pl.ds(pl.multiple_of(half * HALF * W, HALF * W), HALF * W)
    rows = pl.ds(pl.multiple_of(half * HALF, HALF), HALF)
    views = [r.at[:, columns] for r in refs[:-1]] + [refs[-1].at[rows, :]]
    copies = [pltpu.make_async_copy(v, b, sem.at[n]) for n, (v, b) in enumerate(zip(views, bufs))]
    for c in (copies[-1], *copies[:-1]):
        c.start()
    return copies


def states_of(core_ref, k_ref, v_ref, ld_ref, kbuf, vbuf, dbuf, sem, own, put):
    k_in, v_in, d_in = load(core_ref, (k_ref, v_ref, ld_ref), (kbuf, vbuf, dbuf), sem, own)
    d_in.wait()
    cum = running(dbuf[...])
    total = cum[:, T - 1 :]
    factor = jnp.exp(total - cum)
    k_in.wait()

    def decayed(j):
        kt = kbuf[:, j * W : (j + 1) * W].T
        return (kt.astype(F32) * factor[j : j + 1, :]).astype(BF)

    ready = [decayed(j) for j in range(READY)]
    v_in.wait()
    for j in range(HALF):
        if j + READY < HALF:
            ready.append(decayed(j + READY))
        put(j, dot(ready[j], vbuf[:, j * W : (j + 1) * W]))
    return jnp.broadcast_to(jnp.exp(total), (HALF, W))


def send_states(core_ref, k_ref, v_ref, ld_ref, out_ref, *scratch):
    def put(j, state):
        out_ref[j * W : (j + 1) * W, :] = state.astype(BF)

    decay = states_of(core_ref, k_ref, v_ref, ld_ref, *scratch, own=False, put=put)
    first = HALF * W
    for n, term in enumerate(split3(decay)):
        out_ref[first + n * HALF : first + (n + 1) * HALF, :] = term.astype(BF)


def own_states(core_ref, k_ref, v_ref, ld_ref, out_ref, decay_ref, *scratch):
    def put(j, state):
        out_ref[j] = state

    decay_ref[...] = states_of(core_ref, k_ref, v_ref, ld_ref, *scratch, own=True, put=put)


def other_decay(recv_ref):
    first = HALF * W
    terms = [recv_ref[first + n * HALF : first + (n + 1) * HALF, :].astype(F32) for n in range(3)]
    return terms[0] + terms[1] + terms[2]


def combine(core_ref, own_ref, decay_ref, recv_ref, out_ref, first_ref, first_decay_ref):
    here = decay_ref[...]
    there = other_decay(recv_ref)
    earlier = core_ref[0] == 0
    one = jnp.ones_like(here)
    a_own = jnp.where(earlier, there, one)
    a_recv = jnp.where(earlier, one, here)
    first_decay_ref[...] = jnp.where(earlier, here, there)
    terms = split3(here * there)
    zeros = jnp.zeros((ROWS - 32 - 3, W), F32)
    for h in range(HALF):
        tail = jnp.concatenate([t[h : h + 1] for t in terms] + [zeros], axis=0)
        for r in range(4):
            rows = slice(r * 32, (r + 1) * 32)
            own = own_ref[h, rows, :]
            recv = recv_ref[h * W + r * 32 : h * W + (r + 1) * 32, :].astype(F32)
            body = a_own[h : h + 1] * own + a_recv[h : h + 1] * recv
            out_ref[4 * h + r] = jnp.concatenate([body, tail], axis=0).astype(BF)
            first_ref[h, rows, :] = jnp.where(earlier, own, recv).astype(BF)


def scan_chips(in_ref, out_ref):
    carry = jnp.zeros((32, W), F32)
    for j in range(in_ref.shape[0]):
        out_ref[j] = carry.astype(BF)
        x = in_ref[j].astype(F32)
        decay = x[32:33] + x[33:34] + x[34:35]
        carry = decay * carry + x[:32]


def spread_back(core_ref, near_ref, chip_ref, first_ref, first_decay_ref, keep_ref, send_ref):
    earlier = core_ref[0] == 0
    decay = first_decay_ref[...]
    for h in range(HALF):
        for r in range(4):
            rows = slice(r * 32, (r + 1) * 32)
            first = chip_ref[4 * h + r].astype(F32)
            second = decay[h : h + 1] * first + first_ref[h, rows, :].astype(F32)
            keep_ref[h, rows, :] = jnp.where(earlier, first, second).astype(BF)
            send_ref[h, rows, :] = jnp.where(earlier, second, first).astype(BF)


def within(core_ref, ld_ref, q_ref, k_ref, v_ref, near_ref, far_ref):
    @pl.when(pl.program_id(0) < HALF // HB)
    def _():
        within_step(ld_ref, q_ref, k_ref, v_ref, near_ref)

    @pl.when(pl.program_id(0) >= HALF // HB)
    def _():
        within_step(ld_ref, q_ref, k_ref, v_ref, far_ref)


def within_step(ld_ref, q_ref, k_ref, v_ref, out_ref):
    cum = running(ld_ref[...])
    cols = cum.T
    n = W
    causal = lax.broadcasted_iota(jnp.int32, (n, n), 0) >= lax.broadcasted_iota(jnp.int32, (n, n), 1)

    def scores(j):
        at = slice(j * W, (j + 1) * W)
        nt = ((1,), (1,))
        return dot(q_ref[:n, at], k_ref[:n, at], nt), dot(q_ref[n:, at], k_ref[:, at], nt)

    def weights(j, upper, lower):
        row, col = cum[j : j + 1, :], cols[:, j : j + 1]

        def decay(t, s):
            gap = col[t * n : (t + 1) * n] - row[:, s * n : (s + 1) * n]
            if t == s:
                gap = jnp.where(causal, gap, -1e30)
            return jnp.exp(jnp.minimum(gap, 0.0))

        low = [lower[:, :n] * decay(1, 0), lower[:, n:] * decay(1, 1)]
        return (upper * decay(0, 0)).astype(BF), jnp.concatenate(low, axis=1).astype(BF)

    def total(j, upper, lower):
        at = slice(j * W, (j + 1) * W)
        out_ref[:n, at] = dot(upper, v_ref[:n, at])
        out_ref[n:, at] = dot(lower, v_ref[:, at])

    following = scores(0)
    waiting = None
    for j in range(HB):
        current = following
        if j + 1 < HB:
            following = scores(j + 1)
        made = weights(j, *current)
        if waiting is not None:
            total(j - 1, *waiting)
        waiting = made
    total(HB - 1, *waiting)


def finish_half(half, ld_ref, q_ref, inner_ref, carried_ref, gain_ref, put):
    grown = jnp.exp(running(ld_ref[pl.ds(pl.multiple_of(half * HALF, HALF), HALF), :])).T
    ones = jnp.full((W, W), 1.0 / W, BF)

    def columns(j):
        return pl.ds(pl.multiple_of(half * HALF * W + j * W, W), W)

    def readout(j):
        return dot(q_ref[:, columns(j)], carried_ref[j])

    ready = [readout(j) for j in range(AHEAD)]
    for j in range(HALF):
        if j + AHEAD < HALF:
            ready.append(readout(j + AHEAD))
        at = slice(j * W, (j + 1) * W)
        numer = inner_ref[:, at] + ready[j] * grown[:, j : j + 1]
        mean = dot((numer * numer).astype(BF), ones)
        put(j, (numer * lax.rsqrt(mean + 1e-6) * gain_ref[:, columns(j)]).astype(BF))


def finish_own(core_ref, ld_ref, q_ref, inner_ref, carried_ref, gain_ref, out_ref):
    def put(j, value):
        out_ref[:, j * W : (j + 1) * W] = value

    finish_half(core_ref[0], ld_ref, q_ref, inner_ref, carried_ref, gain_ref, put)


def finish_other(core_ref, own_ref, ld_ref, q_ref, inner_ref, carried_ref, gain_ref, out_ref, buf, sem):
    half = 1 - core_ref[0]
    first = pl.ds(pl.multiple_of(core_ref[0] * HALF * W, HALF * W), HALF * W)
    copies = [pltpu.make_async_copy(own_ref, out_ref.at[:, first], sem.at[HALF // PART])]
    copies[0].start()

    def put(j, value):
        buf[:, j * W : (j + 1) * W] = value
        if j % PART == PART - 1:
            at = j + 1 - PART
            to = pl.ds(pl.multiple_of(half * HALF * W + at * W, W), PART * W)
            copy = pltpu.make_async_copy(buf.at[:, at * W : (j + 1) * W], out_ref.at[:, to], sem.at[j // PART])
            copy.start()
            copies.append(copy)

    finish_half(half, ld_ref, q_ref, inner_ref, carried_ref, gain_ref, put)
    for copy in copies:
        copy.wait()


def cost(flops, bytes_accessed):
    return pl.CostEstimate(flops=flops, bytes_accessed=bytes_accessed, transcendentals=0)


def call(kernel, ins, outs, shapes, scratch=(), limit=LIMIT, **kw):
    return pl.pallas_call(
        kernel,
        in_specs=ins,
        out_specs=outs,
        out_shape=shapes,
        scratch_shapes=list(scratch),
        compiler_params=pltpu.CompilerParams(vmem_limit_bytes=limit * MB),
        **kw,
    )


def within_blocks(which, *arrays):
    groups = 2 * HALF // HB

    def group(i, core):
        return (core[0] * (HALF // HB) + i) % groups

    return pl.pallas_call(
        within,
        grid_spec=pltpu.PrefetchScalarGridSpec(
            num_scalar_prefetch=1,
            grid=(groups,),
            in_specs=[pl.BlockSpec((HB, T), lambda i, c: (group(i, c), 0))]
            + [pl.BlockSpec((T, HB * W), lambda i, c: (0, group(i, c)))] * 3,
            out_specs=[
                pl.BlockSpec((T, HB * W), lambda i, c: (0, jnp.minimum(i, groups // 2 - 1))),
                pl.BlockSpec((T, HB * W), lambda i, c: (0, jnp.maximum(i - groups // 2, 0))),
            ],
        ),
        out_shape=[pltpu.HBM((T, HALF * W), F32)] * 2,
        compiler_params=pltpu.CompilerParams(vmem_limit_bytes=LIMIT * MB),
        cost_estimate=cost(1 << 31, 10 * MB),
    )(which, *arrays)


def on_device(queries, keys, values, log_decay, gain):
    which = lax.axis_index("c").astype(jnp.int32).reshape(1)
    heads = log_decay.shape[0]
    chips = HALF * 4
    smem = pl.BlockSpec(memory_space=pltpu.SMEM)
    vmem = pl.BlockSpec(memory_space=pltpu.VMEM)
    hbm = pl.BlockSpec(memory_space=pltpu.HBM)
    struct = jax.ShapeDtypeStruct
    far_q, far_k, far_v, far_ld = (
        pltpu.with_memory_space_constraint(a, pltpu.HBM) for a in (queries, keys, values, log_decay)
    )
    swap = functools.partial(lax.ppermute, axis_name="c", perm=[(0, 1), (1, 0)])
    halves = [
        pltpu.VMEM((T, HALF * W), BF),
        pltpu.VMEM((T, HALF * W), BF),
        pltpu.VMEM((HALF, T), F32),
        pltpu.SemaphoreType.DMA((3,)),
    ]
    sources = (which, far_k, far_v, far_ld)
    sent = call(
        send_states, [smem, hbm, hbm, hbm], vmem, struct((HALF * W + SPLIT, W), BF), halves,
        cost_estimate=cost(1 << 27, 3 * MB),
    )(*sources)
    recv = swap(sent)
    state, decay = call(
        own_states, [smem, hbm, hbm, hbm], [vmem, vmem],
        [struct((HALF, W, W), F32), struct((HALF, W), F32)], halves,
        cost_estimate=cost(1 << 27, 3 * MB),
    )(*sources)
    chunks, first, first_decay = call(
        combine, [smem, vmem, vmem, vmem], [vmem] * 3,
        [struct((chips, ROWS, W), BF), struct((HALF, W, W), BF), struct((HALF, W), F32)],
    )(which, state, decay, recv)
    chunks, far_q = lax.optimization_barrier((chunks, far_q))
    owned = lax.all_to_all(chunks, CHIPS, split_axis=0, concat_axis=0, tiled=True)
    near, far = within_blocks(which, far_ld, far_q, far_k, far_v)
    owned, near, far = lax.optimization_barrier((owned, near, far))
    before = call(scan_chips, [vmem], vmem, struct((chips, 32, W), BF), cost_estimate=cost(1 << 10, 1 << 10))(owned)
    back = lax.all_to_all(before, CHIPS, split_axis=0, concat_axis=0, tiled=True)
    keep, give = call(
        spread_back, [smem, vmem, vmem, vmem, vmem], [vmem] * 2, [struct((HALF, W, W), BF)] * 2,
        cost_estimate=cost(1 << 10, 1 << 10),
    )(which, near, back, first, first_decay)
    taken = swap(give)
    gains = gain.reshape(1, heads * W)
    started = call(
        finish_own, [smem] + [vmem] * 5, vmem, struct((T, HALF * W), BF), limit=FINISH,
        cost_estimate=cost(1 << 27, 5 * MB),
    )(which, log_decay, queries, near, keep, gains)
    return call(
        finish_other, [smem] + [vmem] * 6, hbm, pltpu.HBM((T, heads * W), BF),
        [pltpu.VMEM((T, HALF * W), BF), pltpu.SemaphoreType.DMA((HALF // PART + 1,))], FINISH,
        cost_estimate=cost(1 << 27, 5 * MB),
    )(which, started, log_decay, queries, far, taken, gains)


def solution(mesh):
    chips = Mesh(mesh.devices.reshape(4, 4, 4, 2), ALL)
    placed = (P(ALL, None), P(ALL, None), P(ALL, None), P(None, ALL), P())
    return jax.shard_map(on_device, mesh=chips, in_specs=placed, out_specs=P(ALL, None), check_vma=False)
```

```python
import functools

import jax
import jax.numpy as jnp
from jax import lax
from jax.experimental import pallas as pl
from jax.experimental.pallas import tpu as pltpu
from jax.sharding import Mesh
from jax.sharding import PartitionSpec as P

BF = jnp.bfloat16
F32 = jnp.float32
CHIPS = ("z", "y", "x")
ALL = ("z", "y", "x", "c")
HB = 8
W = 128
T = 256
HALF = 16
SPLIT = 48
ROWS = 40
AHEAD = 1
READY = 4
PART = 4
MB = 1 << 20
LIMIT = 12
FINISH = 20


def running(x):
    lane = lax.broadcasted_iota(jnp.int32, x.shape, 1)
    step = 1
    while step < x.shape[1]:
        x = x + jnp.where(lane >= step, pltpu.roll(x, step, axis=1), 0.0)
        step *= 2
    return x


def split3(x):
    hi = x.astype(BF).astype(F32)
    mid = (x - hi).astype(BF).astype(F32)
    return hi, mid, x - hi - mid


def dot(a, b, dims=((1,), (0,))):
    return lax.dot_general(a, b, (dims, ((), ())), preferred_element_type=F32)


def load(core_ref, refs, bufs, sem, own):
    half = core_ref[0] if own else 1 - core_ref[0]
    columns = pl.ds(pl.multiple_of(half * HALF * W, HALF * W), HALF * W)
    rows = pl.ds(pl.multiple_of(half * HALF, HALF), HALF)
    views = [r.at[:, columns] for r in refs[:-1]] + [refs[-1].at[rows, :]]
    copies = [pltpu.make_async_copy(v, b, sem.at[n]) for n, (v, b) in enumerate(zip(views, bufs))]
    for c in (copies[-1], *copies[:-1]):
        c.start()
    return copies


def states_of(core_ref, k_ref, v_ref, ld_ref, kbuf, vbuf, dbuf, sem, own, put):
    k_in, v_in, d_in = load(core_ref, (k_ref, v_ref, ld_ref), (kbuf, vbuf, dbuf), sem, own)
    d_in.wait()
    cum = running(dbuf[...])
    total = cum[:, T - 1 :]
    factor = jnp.exp(total - cum)
    k_in.wait()

    def decayed(j):
        kt = kbuf[:, j * W : (j + 1) * W].T
        return (kt.astype(F32) * factor[j : j + 1, :]).astype(BF)

    ready = [decayed(j) for j in range(READY)]
    v_in.wait()
    for j in range(HALF):
        if j + READY < HALF:
            ready.append(decayed(j + READY))
        put(j, dot(ready[j], vbuf[:, j * W : (j + 1) * W]))
    return jnp.broadcast_to(jnp.exp(total), (HALF, W))


def send_states(core_ref, k_ref, v_ref, ld_ref, out_ref, *scratch):
    def put(j, state):
        out_ref[j * W : (j + 1) * W, :] = state.astype(BF)

    decay = states_of(core_ref, k_ref, v_ref, ld_ref, *scratch, own=False, put=put)
    first = HALF * W
    for n, term in enumerate(split3(decay)):
        out_ref[first + n * HALF : first + (n + 1) * HALF, :] = term.astype(BF)


def own_states(core_ref, k_ref, v_ref, ld_ref, out_ref, decay_ref, *scratch):
    def put(j, state):
        out_ref[j] = state

    decay_ref[...] = states_of(core_ref, k_ref, v_ref, ld_ref, *scratch, own=True, put=put)


def other_decay(recv_ref):
    first = HALF * W
    terms = [recv_ref[first + n * HALF : first + (n + 1) * HALF, :].astype(F32) for n in range(3)]
    return terms[0] + terms[1] + terms[2]


def combine(core_ref, own_ref, decay_ref, recv_ref, out_ref, first_ref, first_decay_ref):
    here = decay_ref[...]
    there = other_decay(recv_ref)
    earlier = core_ref[0] == 0
    one = jnp.ones_like(here)
    a_own = jnp.where(earlier, there, one)
    a_recv = jnp.where(earlier, one, here)
    first_decay_ref[...] = jnp.where(earlier, here, there)
    terms = split3(here * there)
    zeros = jnp.zeros((ROWS - 32 - 3, W), F32)
    for h in range(HALF):
        tail = jnp.concatenate([t[h : h + 1] for t in terms] + [zeros], axis=0)
        for r in range(4):
            rows = slice(r * 32, (r + 1) * 32)
            own = own_ref[h, rows, :]
            recv = recv_ref[h * W + r * 32 : h * W + (r + 1) * 32, :].astype(F32)
            body = a_own[h : h + 1] * own + a_recv[h : h + 1] * recv
            out_ref[4 * h + r] = jnp.concatenate([body, tail], axis=0).astype(BF)
            first_ref[h, rows, :] = jnp.where(earlier, own, recv).astype(BF)


def scan_chips(in_ref, out_ref):
    carry = jnp.zeros((32, W), F32)
    for j in range(in_ref.shape[0]):
        out_ref[j] = carry.astype(BF)
        x = in_ref[j].astype(F32)
        decay = x[32:33] + x[33:34] + x[34:35]
        carry = decay * carry + x[:32]


def before_block(chip_ref, first_ref, decay, wants_first, h):
    first = chip_ref[4 * h : 4 * h + 4].reshape(W, W).astype(F32)
    second = decay[h : h + 1] * first + first_ref[h].astype(F32)
    return jnp.where(wants_first, first, second).astype(BF)


def spread_back(core_ref, near_ref, chip_ref, first_ref, first_decay_ref, send_ref):
    decay = first_decay_ref[...]
    for h in range(HALF):
        send_ref[h] = before_block(chip_ref, first_ref, decay, core_ref[0] != 0, h)


def within(core_ref, ld_ref, q_ref, k_ref, v_ref, near_ref, far_ref):
    @pl.when(pl.program_id(0) < HALF // HB)
    def _():
        within_step(ld_ref, q_ref, k_ref, v_ref, near_ref)

    @pl.when(pl.program_id(0) >= HALF // HB)
    def _():
        within_step(ld_ref, q_ref, k_ref, v_ref, far_ref)


def within_step(ld_ref, q_ref, k_ref, v_ref, out_ref):
    cum = running(ld_ref[...])
    cols = cum.T
    n = W
    causal = lax.broadcasted_iota(jnp.int32, (n, n), 0) >= lax.broadcasted_iota(jnp.int32, (n, n), 1)

    def scores(j):
        at = slice(j * W, (j + 1) * W)
        nt = ((1,), (1,))
        return dot(q_ref[:n, at], k_ref[:n, at], nt), dot(q_ref[n:, at], k_ref[:, at], nt)

    def weights(j, upper, lower):
        row, col = cum[j : j + 1, :], cols[:, j : j + 1]

        def decay(t, s):
            gap = col[t * n : (t + 1) * n] - row[:, s * n : (s + 1) * n]
            if t == s:
                gap = jnp.where(causal, gap, -1e30)
            return jnp.exp(jnp.minimum(gap, 0.0))

        low = [lower[:, :n] * decay(1, 0), lower[:, n:] * decay(1, 1)]
        return (upper * decay(0, 0)).astype(BF), jnp.concatenate(low, axis=1).astype(BF)

    def total(j, upper, lower):
        at = slice(j * W, (j + 1) * W)
        out_ref[:n, at] = dot(upper, v_ref[:n, at])
        out_ref[n:, at] = dot(lower, v_ref[:, at])

    following = scores(0)
    waiting = None
    for j in range(HB):
        current = following
        if j + 1 < HB:
            following = scores(j + 1)
        made = weights(j, *current)
        if waiting is not None:
            total(j - 1, *waiting)
        waiting = made
    total(HB - 1, *waiting)


def finish_half(half, ld_ref, q_ref, inner_ref, carried, gain_ref, put):
    grown = jnp.exp(running(ld_ref[pl.ds(pl.multiple_of(half * HALF, HALF), HALF), :])).T
    ones = jnp.full((W, W), 1.0 / W, BF)

    def columns(j):
        return pl.ds(pl.multiple_of(half * HALF * W + j * W, W), W)

    def readout(j):
        return dot(q_ref[:, columns(j)], carried(j))

    ready = [readout(j) for j in range(AHEAD)]
    for j in range(HALF):
        if j + AHEAD < HALF:
            ready.append(readout(j + AHEAD))
        at = slice(j * W, (j + 1) * W)
        numer = inner_ref[:, at] + ready[j] * grown[:, j : j + 1]
        mean = dot((numer * numer).astype(BF), ones)
        put(j, (numer * lax.rsqrt(mean + 1e-6) * gain_ref[:, columns(j)]).astype(BF))


def finish_own(core_ref, ld_ref, q_ref, inner_ref, chip_ref, first_ref, first_decay_ref, gain_ref, out_ref):
    decay = first_decay_ref[...]

    def carried(j):
        return before_block(chip_ref, first_ref, decay, core_ref[0] == 0, j)

    def put(j, value):
        out_ref[:, j * W : (j + 1) * W] = value

    finish_half(core_ref[0], ld_ref, q_ref, inner_ref, carried, gain_ref, put)


def finish_other(core_ref, own_ref, ld_ref, q_ref, inner_ref, carried_ref, gain_ref, out_ref, buf, sem):
    half = 1 - core_ref[0]
    first = pl.ds(pl.multiple_of(core_ref[0] * HALF * W, HALF * W), HALF * W)
    copies = [pltpu.make_async_copy(own_ref, out_ref.at[:, first], sem.at[HALF // PART])]
    copies[0].start()

    def put(j, value):
        buf[:, j * W : (j + 1) * W] = value
        if j % PART == PART - 1:
            at = j + 1 - PART
            to = pl.ds(pl.multiple_of(half * HALF * W + at * W, W), PART * W)
            copy = pltpu.make_async_copy(buf.at[:, at * W : (j + 1) * W], out_ref.at[:, to], sem.at[j // PART])
            copy.start()
            copies.append(copy)

    finish_half(half, ld_ref, q_ref, inner_ref, lambda j: carried_ref[j], gain_ref, put)
    for copy in copies:
        copy.wait()


def cost(flops, bytes_accessed):
    return pl.CostEstimate(flops=flops, bytes_accessed=bytes_accessed, transcendentals=0)


def call(kernel, ins, outs, shapes, scratch=(), limit=LIMIT, **kw):
    return pl.pallas_call(
        kernel,
        in_specs=ins,
        out_specs=outs,
        out_shape=shapes,
        scratch_shapes=list(scratch),
        compiler_params=pltpu.CompilerParams(vmem_limit_bytes=limit * MB),
        **kw,
    )


def within_blocks(which, *arrays):
    groups = 2 * HALF // HB

    def group(i, core):
        return (core[0] * (HALF // HB) + i) % groups

    return pl.pallas_call(
        within,
        grid_spec=pltpu.PrefetchScalarGridSpec(
            num_scalar_prefetch=1,
            grid=(groups,),
            in_specs=[pl.BlockSpec((HB, T), lambda i, c: (group(i, c), 0))]
            + [pl.BlockSpec((T, HB * W), lambda i, c: (0, group(i, c)))] * 3,
            out_specs=[
                pl.BlockSpec((T, HB * W), lambda i, c: (0, jnp.minimum(i, groups // 2 - 1))),
                pl.BlockSpec((T, HB * W), lambda i, c: (0, jnp.maximum(i - groups // 2, 0))),
            ],
        ),
        out_shape=[pltpu.HBM((T, HALF * W), F32)] * 2,
        compiler_params=pltpu.CompilerParams(vmem_limit_bytes=LIMIT * MB),
        cost_estimate=cost(1 << 31, 10 * MB),
    )(which, *arrays)


def on_device(queries, keys, values, log_decay, gain):
    which = lax.axis_index("c").astype(jnp.int32).reshape(1)
    heads = log_decay.shape[0]
    chips = HALF * 4
    smem = pl.BlockSpec(memory_space=pltpu.SMEM)
    vmem = pl.BlockSpec(memory_space=pltpu.VMEM)
    hbm = pl.BlockSpec(memory_space=pltpu.HBM)
    struct = jax.ShapeDtypeStruct
    far_q, far_k, far_v, far_ld = (
        pltpu.with_memory_space_constraint(a, pltpu.HBM) for a in (queries, keys, values, log_decay)
    )
    swap = functools.partial(lax.ppermute, axis_name="c", perm=[(0, 1), (1, 0)])
    halves = [
        pltpu.VMEM((T, HALF * W), BF),
        pltpu.VMEM((T, HALF * W), BF),
        pltpu.VMEM((HALF, T), F32),
        pltpu.SemaphoreType.DMA((3,)),
    ]
    sources = (which, far_k, far_v, far_ld)
    sent = call(
        send_states, [smem, hbm, hbm, hbm], vmem, struct((HALF * W + SPLIT, W), BF), halves,
        cost_estimate=cost(1 << 27, 3 * MB),
    )(*sources)
    recv = swap(sent)
    state, decay = call(
        own_states, [smem, hbm, hbm, hbm], [vmem, vmem],
        [struct((HALF, W, W), F32), struct((HALF, W), F32)], halves,
        cost_estimate=cost(1 << 27, 3 * MB),
    )(*sources)
    chunks, first, first_decay = call(
        combine, [smem, vmem, vmem, vmem], [vmem] * 3,
        [struct((chips, ROWS, W), BF), struct((HALF, W, W), BF), struct((HALF, W), F32)],
    )(which, state, decay, recv)
    chunks, far_q = lax.optimization_barrier((chunks, far_q))
    owned = lax.all_to_all(chunks, CHIPS, split_axis=0, concat_axis=0, tiled=True)
    near, far = within_blocks(which, far_ld, far_q, far_k, far_v)
    owned, near, far = lax.optimization_barrier((owned, near, far))
    before = call(scan_chips, [vmem], vmem, struct((chips, 32, W), BF), cost_estimate=cost(1 << 10, 1 << 10))(owned)
    back = lax.all_to_all(before, CHIPS, split_axis=0, concat_axis=0, tiled=True)
    give = call(
        spread_back, [smem, vmem, vmem, vmem, vmem], vmem, struct((HALF, W, W), BF),
        cost_estimate=cost(1 << 10, 1 << 10),
    )(which, near, back, first, first_decay)
    taken = swap(give)
    gains = gain.reshape(1, heads * W)
    started = call(
        finish_own, [smem] + [vmem] * 7, vmem, struct((T, HALF * W), BF), limit=FINISH,
        cost_estimate=cost(1 << 27, 5 * MB),
    )(which, log_decay, queries, near, back, first, first_decay, gains)
    return call(
        finish_other, [smem] + [vmem] * 6, hbm, pltpu.HBM((T, heads * W), BF),
        [pltpu.VMEM((T, HALF * W), BF), pltpu.SemaphoreType.DMA((HALF // PART + 1,))], FINISH,
        cost_estimate=cost(1 << 27, 5 * MB),
    )(which, started, log_decay, queries, far, taken, gains)


def solution(mesh):
    chips = Mesh(mesh.devices.reshape(4, 4, 4, 2), ALL)
    placed = (P(ALL, None), P(ALL, None), P(ALL, None), P(None, ALL), P())
    return jax.shard_map(on_device, mesh=chips, in_specs=placed, out_specs=P(ALL, None), check_vma=False)
```

```python
import functools

import jax
import jax.numpy as jnp
from jax import lax
from jax.experimental import pallas as pl
from jax.experimental.pallas import tpu as pltpu
from jax.sharding import Mesh
from jax.sharding import PartitionSpec as P

BF = jnp.bfloat16
F32 = jnp.float32
CHIPS = ("z", "y", "x")
ALL = ("z", "y", "x", "c")
HB = 8
W = 128
T = 256
HALF = 16
SPLIT = 48
ROWS = 40
AHEAD = 1
READY = 8
PART = 4
MB = 1 << 20
LIMIT = 12
FINISH = 20


def running(x):
    lane = lax.broadcasted_iota(jnp.int32, x.shape, 1)
    step = 1
    while step < x.shape[1]:
        x = x + jnp.where(lane >= step, pltpu.roll(x, step, axis=1), 0.0)
        step *= 2
    return x


def split3(x):
    hi = x.astype(BF).astype(F32)
    mid = (x - hi).astype(BF).astype(F32)
    return hi, mid, x - hi - mid


def dot(a, b, dims=((1,), (0,))):
    return lax.dot_general(a, b, (dims, ((), ())), preferred_element_type=F32)


def load(core_ref, refs, bufs, sem, own):
    half = core_ref[0] if own else 1 - core_ref[0]
    columns = pl.ds(pl.multiple_of(half * HALF * W, HALF * W), HALF * W)
    rows = pl.ds(pl.multiple_of(half * HALF, HALF), HALF)
    views = [r.at[:, columns] for r in refs[:-1]] + [refs[-1].at[rows, :]]
    copies = [pltpu.make_async_copy(v, b, sem.at[n]) for n, (v, b) in enumerate(zip(views, bufs))]
    for c in (copies[-1], *copies[:-1]):
        c.start()
    return copies


def states_of(core_ref, k_ref, v_ref, ld_ref, kbuf, vbuf, dbuf, sem, own, put):
    k_in, v_in, d_in = load(core_ref, (k_ref, v_ref, ld_ref), (kbuf, vbuf, dbuf), sem, own)
    d_in.wait()
    cum = running(dbuf[...])
    total = cum[:, T - 1 :]
    factor = jnp.exp(total - cum)
    k_in.wait()

    def decayed(j):
        kt = kbuf[:, j * W : (j + 1) * W].T
        return (kt.astype(F32) * factor[j : j + 1, :]).astype(BF)

    ready = [decayed(j) for j in range(READY)]
    v_in.wait()
    for j in range(HALF):
        if j + READY < HALF:
            ready.append(decayed(j + READY))
        put(j, dot(ready[j], vbuf[:, j * W : (j + 1) * W]))
    return jnp.broadcast_to(jnp.exp(total), (HALF, W))


def send_states(core_ref, k_ref, v_ref, ld_ref, out_ref, *scratch):
    def put(j, state):
        out_ref[j * W : (j + 1) * W, :] = state.astype(BF)

    decay = states_of(core_ref, k_ref, v_ref, ld_ref, *scratch, own=False, put=put)
    first = HALF * W
    for n, term in enumerate(split3(decay)):
        out_ref[first + n * HALF : first + (n + 1) * HALF, :] = term.astype(BF)


def own_states(core_ref, k_ref, v_ref, ld_ref, out_ref, decay_ref, *scratch):
    def put(j, state):
        out_ref[j] = state

    decay_ref[...] = states_of(core_ref, k_ref, v_ref, ld_ref, *scratch, own=True, put=put)


def other_decay(recv_ref):
    first = HALF * W
    terms = [recv_ref[first + n * HALF : first + (n + 1) * HALF, :].astype(F32) for n in range(3)]
    return terms[0] + terms[1] + terms[2]


def combine(core_ref, own_ref, decay_ref, recv_ref, out_ref, first_ref, first_decay_ref):
    here = decay_ref[...]
    there = other_decay(recv_ref)
    earlier = core_ref[0] == 0
    one = jnp.ones_like(here)
    a_own = jnp.where(earlier, there, one)
    a_recv = jnp.where(earlier, one, here)
    first_decay_ref[...] = jnp.where(earlier, here, there)
    terms = split3(here * there)
    zeros = jnp.zeros((ROWS - 32 - 3, W), F32)
    for h in range(HALF):
        tail = jnp.concatenate([t[h : h + 1] for t in terms] + [zeros], axis=0)
        for r in range(4):
            rows = slice(r * 32, (r + 1) * 32)
            own = own_ref[h, rows, :]
            recv = recv_ref[h * W + r * 32 : h * W + (r + 1) * 32, :].astype(F32)
            body = a_own[h : h + 1] * own + a_recv[h : h + 1] * recv
            out_ref[4 * h + r] = jnp.concatenate([body, tail], axis=0).astype(BF)
            first_ref[h, rows, :] = jnp.where(earlier, own, recv).astype(BF)


def scan_chips(in_ref, out_ref):
    carry = jnp.zeros((32, W), F32)
    for j in range(in_ref.shape[0]):
        out_ref[j] = carry.astype(BF)
        x = in_ref[j].astype(F32)
        decay = x[32:33] + x[33:34] + x[34:35]
        carry = decay * carry + x[:32]


def before_block(chip_ref, first_ref, decay, wants_first, h):
    first = chip_ref[4 * h : 4 * h + 4].reshape(W, W).astype(F32)
    second = decay[h : h + 1] * first + first_ref[h].astype(F32)
    return jnp.where(wants_first, first, second).astype(BF)


def spread_back(core_ref, near_ref, chip_ref, first_ref, first_decay_ref, send_ref):
    decay = first_decay_ref[...]
    for h in range(HALF):
        send_ref[h] = before_block(chip_ref, first_ref, decay, core_ref[0] != 0, h)


def within(core_ref, ld_ref, q_ref, k_ref, v_ref, near_ref, far_ref):
    @pl.when(pl.program_id(0) < HALF // HB)
    def _():
        within_step(ld_ref, q_ref, k_ref, v_ref, near_ref)

    @pl.when(pl.program_id(0) >= HALF // HB)
    def _():
        within_step(ld_ref, q_ref, k_ref, v_ref, far_ref)


def within_step(ld_ref, q_ref, k_ref, v_ref, out_ref):
    cum = running(ld_ref[...])
    cols = cum.T
    n = W
    causal = lax.broadcasted_iota(jnp.int32, (n, n), 0) >= lax.broadcasted_iota(jnp.int32, (n, n), 1)

    def scores(j):
        at = slice(j * W, (j + 1) * W)
        nt = ((1,), (1,))
        return dot(q_ref[:n, at], k_ref[:n, at], nt), dot(q_ref[n:, at], k_ref[:, at], nt)

    def weights(j, upper, lower):
        row, col = cum[j : j + 1, :], cols[:, j : j + 1]

        def decay(t, s):
            gap = col[t * n : (t + 1) * n] - row[:, s * n : (s + 1) * n]
            if t == s:
                gap = jnp.where(causal, gap, -1e30)
            return jnp.exp(jnp.minimum(gap, 0.0))

        low = [lower[:, :n] * decay(1, 0), lower[:, n:] * decay(1, 1)]
        return (upper * decay(0, 0)).astype(BF), jnp.concatenate(low, axis=1).astype(BF)

    def total(j, upper, lower):
        at = slice(j * W, (j + 1) * W)
        out_ref[:n, at] = dot(upper, v_ref[:n, at])
        out_ref[n:, at] = dot(lower, v_ref[:, at])

    following = scores(0)
    waiting = None
    for j in range(HB):
        current = following
        if j + 1 < HB:
            following = scores(j + 1)
        made = weights(j, *current)
        if waiting is not None:
            total(j - 1, *waiting)
        waiting = made
    total(HB - 1, *waiting)


def finish_half(half, ld_ref, q_ref, inner_ref, carried, gain_ref, put):
    grown = jnp.exp(running(ld_ref[pl.ds(pl.multiple_of(half * HALF, HALF), HALF), :])).T
    ones = jnp.full((W, W), 1.0 / W, BF)

    def columns(j):
        return pl.ds(pl.multiple_of(half * HALF * W + j * W, W), W)

    def readout(j):
        return dot(q_ref[:, columns(j)], carried(j))

    ready = [readout(j) for j in range(AHEAD)]
    for j in range(HALF):
        if j + AHEAD < HALF:
            ready.append(readout(j + AHEAD))
        at = slice(j * W, (j + 1) * W)
        numer = inner_ref[:, at] + ready[j] * grown[:, j : j + 1]
        mean = dot((numer * numer).astype(BF), ones)
        put(j, (numer * lax.rsqrt(mean + 1e-6) * gain_ref[:, columns(j)]).astype(BF))


def finish_own(core_ref, ld_ref, q_ref, inner_ref, chip_ref, first_ref, first_decay_ref, gain_ref, out_ref):
    decay = first_decay_ref[...]

    def carried(j):
        return before_block(chip_ref, first_ref, decay, core_ref[0] == 0, j)

    def put(j, value):
        out_ref[:, j * W : (j + 1) * W] = value

    finish_half(core_ref[0], ld_ref, q_ref, inner_ref, carried, gain_ref, put)


def finish_other(core_ref, own_ref, ld_ref, q_ref, inner_ref, carried_ref, gain_ref, out_ref, buf, sem):
    half = 1 - core_ref[0]
    first = pl.ds(pl.multiple_of(core_ref[0] * HALF * W, HALF * W), HALF * W)
    copies = [pltpu.make_async_copy(own_ref, out_ref.at[:, first], sem.at[HALF // PART])]
    copies[0].start()

    def put(j, value):
        buf[:, j * W : (j + 1) * W] = value
        if j % PART == PART - 1:
            at = j + 1 - PART
            to = pl.ds(pl.multiple_of(half * HALF * W + at * W, W), PART * W)
            copy = pltpu.make_async_copy(buf.at[:, at * W : (j + 1) * W], out_ref.at[:, to], sem.at[j // PART])
            copy.start()
            copies.append(copy)

    finish_half(half, ld_ref, q_ref, inner_ref, lambda j: carried_ref[j], gain_ref, put)
    for copy in copies:
        copy.wait()


def cost(flops, bytes_accessed):
    return pl.CostEstimate(flops=flops, bytes_accessed=bytes_accessed, transcendentals=0)


def call(kernel, ins, outs, shapes, scratch=(), limit=LIMIT, **kw):
    return pl.pallas_call(
        kernel,
        in_specs=ins,
        out_specs=outs,
        out_shape=shapes,
        scratch_shapes=list(scratch),
        compiler_params=pltpu.CompilerParams(vmem_limit_bytes=limit * MB),
        **kw,
    )


def within_blocks(which, *arrays):
    groups = 2 * HALF // HB

    def group(i, core):
        return (core[0] * (HALF // HB) + i) % groups

    return pl.pallas_call(
        within,
        grid_spec=pltpu.PrefetchScalarGridSpec(
            num_scalar_prefetch=1,
            grid=(groups,),
            in_specs=[pl.BlockSpec((HB, T), lambda i, c: (group(i, c), 0))]
            + [pl.BlockSpec((T, HB * W), lambda i, c: (0, group(i, c)))] * 3,
            out_specs=[
                pl.BlockSpec((T, HB * W), lambda i, c: (0, jnp.minimum(i, groups // 2 - 1))),
                pl.BlockSpec((T, HB * W), lambda i, c: (0, jnp.maximum(i - groups // 2, 0))),
            ],
        ),
        out_shape=[pltpu.HBM((T, HALF * W), F32)] * 2,
        compiler_params=pltpu.CompilerParams(vmem_limit_bytes=LIMIT * MB),
        cost_estimate=cost(1 << 31, 10 * MB),
    )(which, *arrays)


def on_device(queries, keys, values, log_decay, gain):
    which = lax.axis_index("c").astype(jnp.int32).reshape(1)
    heads = log_decay.shape[0]
    chips = HALF * 4
    smem = pl.BlockSpec(memory_space=pltpu.SMEM)
    vmem = pl.BlockSpec(memory_space=pltpu.VMEM)
    hbm = pl.BlockSpec(memory_space=pltpu.HBM)
    struct = jax.ShapeDtypeStruct
    far_q, far_k, far_v, far_ld = (
        pltpu.with_memory_space_constraint(a, pltpu.HBM) for a in (queries, keys, values, log_decay)
    )
    swap = functools.partial(lax.ppermute, axis_name="c", perm=[(0, 1), (1, 0)])
    halves = [
        pltpu.VMEM((T, HALF * W), BF),
        pltpu.VMEM((T, HALF * W), BF),
        pltpu.VMEM((HALF, T), F32),
        pltpu.SemaphoreType.DMA((3,)),
    ]
    sources = (which, far_k, far_v, far_ld)
    sent = call(
        send_states, [smem, hbm, hbm, hbm], vmem, struct((HALF * W + SPLIT, W), BF), halves,
        cost_estimate=cost(1 << 27, 3 * MB),
    )(*sources)
    recv = swap(sent)
    state, decay = call(
        own_states, [smem, hbm, hbm, hbm], [vmem, vmem],
        [struct((HALF, W, W), F32), struct((HALF, W), F32)], halves,
        cost_estimate=cost(1 << 27, 3 * MB),
    )(*sources)
    chunks, first, first_decay = call(
        combine, [smem, vmem, vmem, vmem], [vmem] * 3,
        [struct((chips, ROWS, W), BF), struct((HALF, W, W), BF), struct((HALF, W), F32)],
    )(which, state, decay, recv)
    chunks, far_q = lax.optimization_barrier((chunks, far_q))
    owned = lax.all_to_all(chunks, CHIPS, split_axis=0, concat_axis=0, tiled=True)
    near, far = within_blocks(which, far_ld, far_q, far_k, far_v)
    owned, near, far = lax.optimization_barrier((owned, near, far))
    before = call(scan_chips, [vmem], vmem, struct((chips, 32, W), BF), cost_estimate=cost(1 << 10, 1 << 10))(owned)
    back = lax.all_to_all(before, CHIPS, split_axis=0, concat_axis=0, tiled=True)
    give = call(
        spread_back, [smem, vmem, vmem, vmem, vmem], vmem, struct((HALF, W, W), BF),
        cost_estimate=cost(1 << 10, 1 << 10),
    )(which, near, back, first, first_decay)
    taken = swap(give)
    gains = gain.reshape(1, heads * W)
    started = call(
        finish_own, [smem] + [vmem] * 7, vmem, struct((T, HALF * W), BF), limit=FINISH,
        cost_estimate=cost(1 << 27, 5 * MB),
    )(which, log_decay, queries, near, back, first, first_decay, gains)
    return call(
        finish_other, [smem] + [vmem] * 6, hbm, pltpu.HBM((T, heads * W), BF),
        [pltpu.VMEM((T, HALF * W), BF), pltpu.SemaphoreType.DMA((HALF // PART + 1,))], FINISH,
        cost_estimate=cost(1 << 27, 5 * MB),
    )(which, started, log_decay, queries, far, taken, gains)


def solution(mesh):
    chips = Mesh(mesh.devices.reshape(4, 4, 4, 2), ALL)
    placed = (P(ALL, None), P(ALL, None), P(ALL, None), P(None, ALL), P())
    return jax.shard_map(on_device, mesh=chips, in_specs=placed, out_specs=P(ALL, None), check_vma=False)
```
